32 devices in a mesh: sec: 2 (over x), tp: 4 (over y, core), blk: 4 (over z).
Axes of the slice: x: 2, y: 2, z: 4, core: 2. Of those that a mesh axis runs over, the one named last changes fastest.
Arguments:
- perambulator: bfloat16 [4, 2, 2048, 2048], P('tp', None, 'blk'), may hold values from -0.125 to 0.125
- backward: bfloat16 [4, 2, 2048, 2048], P('tp', None, None, 'blk'), may hold values from -0.125 to 0.125
- elementals: bfloat16 [2, 4, 2, 2048, 128], P('sec', 'tp', None, 'blk'), may hold values from -6 to 6
- diagrams: int32 [4, 16, 2], P('tp'), may hold values from 0 to 3
- owner_loads: int32 [4], P('tp'), may hold values from 1 to 16, as said below
Outputs:
- hadron: float32 [2, 4, 2, 128, 128], P('sec', 'tp', None, 'blk')
The draws below stay inside these ranges and needn't reach their ends.
Inputs may be any that keep to these rules, and one draw needn't show every extreme that they name: `diagrams`: pair indices of each owner's slots; slots at or past the owner's load are ignored. `owner_loads`: some owner has exactly 16 live slots.
All inputs are finite; a program needn't handle non-finite values.
Results may differ from the reference program's by a relative error of at most 0.007.
Values may be sent and summed in bfloat16 or wider, within the bound.
A program may use at most 64 MiB of HBM per device.

```python
import jax
import jax.numpy as jnp
from jax import lax

NS = 2048
K = 128
MAXD = 16
PAIRS = 4
DIAGRAM_HOLDERS = 4
INSERTIONS = 2


def draw_owner_loads(key, part):
    first = jax.random.randint(jax.random.fold_in(key, 11), (DIAGRAM_HOLDERS,), 0, MAXD)
    second = jax.random.randint(jax.random.fold_in(key, 12), (DIAGRAM_HOLDERS,), 0, MAXD)
    piece_count = 1 + first * second // MAXD
    where = jax.random.randint(jax.random.fold_in(key, 13), (), 0, DIAGRAM_HOLDERS)
    return piece_count.at[where].set(MAXD).astype(jnp.int32)


def touch_ends(result, own_key, least, top_value):
    extent = result.shape
    index_at = [jax.random.randint(jax.random.fold_in(own_key, axis), (), 0, extent[axis]) for axis in range(len(extent))]
    result = result.at[tuple(index_at)].set(least)
    longest = extent.index(max(extent))
    index_at[longest] = (index_at[longest] + 1) % extent[longest]
    return result.at[tuple(index_at)].set(top_value)


def steps_of(rng, dims, cuts, smallest, top_value):
    gain, own = 1.0, jax.random.fold_in(rng, 6)
    for axis_at, shards_of in cuts:
        draws = jnp.exp(jax.random.uniform(jax.random.fold_in(own, axis_at), (shards_of,), jnp.float32, smallest / len(cuts), top_value / len(cuts)))
        gain = gain * jnp.repeat(draws, dims[axis_at] // shards_of).reshape([-1 if axis == axis_at else 1 for axis in range(len(dims))])
    return gain


def scatter_about(stream_key, dims, spread, limit, cuts=(), dtype=jnp.bfloat16):
    values = jax.random.normal(stream_key, dims, jnp.float32) * spread
    if len(cuts) > 0:
        values = steps_of(stream_key, dims, cuts, -0.22, 0.18) * values
    return jnp.clip(values, min=-limit, max=limit).astype(dtype)


def setup_inputs(seed: int = 0) -> dict:
    splits = jax.random.split(jax.random.key(seed), 6)
    perambulator = scatter_about(splits[0], (PAIRS, 2, NS, NS), NS ** -0.5, 0.125, ((0, 4), (2, 4)))
    backward = scatter_about(splits[1], (PAIRS, 2, NS, NS), NS ** -0.5, 0.125, ((0, 4), (3, 4)))
    elementals = scatter_about(splits[2], (INSERTIONS, PAIRS, 2, NS, K), 1.0, 6.0, ((0, 2), (1, 4), (3, 4)))
    diagrams = touch_ends(jax.random.randint(splits[3], (DIAGRAM_HOLDERS, MAXD, 2), 0, PAIRS), jax.random.fold_in(splits[3], 1), 0, PAIRS - 1).astype(jnp.int32)
    owner_loads = draw_owner_loads(jax.random.fold_in(splits[5], 71), 0)
    return dict(perambulator=perambulator, backward=backward, elementals=elementals, diagrams=diagrams, owner_loads=owner_loads)


def one_pair(pieces):
    peram_pair, back_pair, pair_tiles = pieces
    tau_real = peram_pair[0].astype(jnp.float32)
    tau_imag = peram_pair[1].astype(jnp.float32)
    back_real = back_pair[0].astype(jnp.float32)
    back_imag = back_pair[1].astype(jnp.float32)
    tile_real = pair_tiles[:, 0].astype(jnp.float32)
    tile_imag = pair_tiles[:, 1].astype(jnp.float32)
    image_real = jnp.einsum('rc,sck->srk', tau_real, tile_real) - jnp.einsum('rc,sck->srk', tau_imag, tile_imag)
    image_imag = jnp.einsum('rc,sck->srk', tau_real, tile_imag) + jnp.einsum('rc,sck->srk', tau_imag, tile_real)
    image_real = image_real.astype(jnp.bfloat16).astype(jnp.float32)
    image_imag = image_imag.astype(jnp.bfloat16).astype(jnp.float32)
    dressed_real = jnp.einsum('ri,sik->srk', back_real, image_real) - jnp.einsum('ri,sik->srk', back_imag, image_imag)
    dressed_imag = jnp.einsum('ri,sik->srk', back_real, image_imag) + jnp.einsum('ri,sik->srk', back_imag, image_real)
    dressed_real = dressed_real.astype(jnp.bfloat16).astype(jnp.float32)
    dressed_imag = dressed_imag.astype(jnp.bfloat16).astype(jnp.float32)
    sink_real = jnp.roll(tile_real, 1, axis=0)
    sink_imag = jnp.roll(tile_imag, 1, axis=0)
    norm_scale = NS ** -0.5
    block_real = (jnp.einsum('sjk,sjm->skm', sink_real, dressed_real) + jnp.einsum('sjk,sjm->skm', sink_imag, dressed_imag)) * norm_scale
    block_imag = (jnp.einsum('sjk,sjm->skm', sink_real, dressed_imag) - jnp.einsum('sjk,sjm->skm', sink_imag, dressed_real)) * norm_scale
    return jnp.stack([block_real, block_imag], axis=1).astype(jnp.bfloat16)


def reference(perambulator, backward, elementals, diagrams, owner_loads):
    blocks = lax.map(one_pair, (perambulator, backward, jnp.moveaxis(elementals, 1, 0)))

    def one_owner(pieces):
        owner_list, owner_load = pieces
        left_blocks = jnp.take(blocks, owner_list[:, 0], axis=0)
        right_blocks = jnp.take(blocks, owner_list[:, 1], axis=0)
        active = (jnp.arange(MAXD) < owner_load).astype(jnp.float32)
        left_float = left_blocks.astype(jnp.float32) * active[:, None, None, None, None]
        right_float = right_blocks.astype(jnp.float32)
        hadron_real = jnp.einsum('gsrk,gskm->srm', left_float[:, :, 0], right_float[:, :, 0]) - jnp.einsum('gsrk,gskm->srm', left_float[:, :, 1], right_float[:, :, 1])
        hadron_imag = jnp.einsum('gsrk,gskm->srm', left_float[:, :, 0], right_float[:, :, 1]) + jnp.einsum('gsrk,gskm->srm', left_float[:, :, 1], right_float[:, :, 0])
        return jnp.stack([hadron_real, hadron_imag], axis=1) * ((K * MAXD) ** -0.5)

    hadron = lax.map(one_owner, (diagrams, owner_loads))
    return jnp.moveaxis(hadron, 0, 1)
```

```python
import functools

import jax
import jax.numpy as jnp
from jax import lax
from jax.experimental import pallas as pl
from jax.experimental.pallas import tpu as pltpu
from jax.sharding import PartitionSpec as P

PARTS = 2
PIECES = 2
MESH = pl.DeviceIdType.MESH


def kernel(
    n_sec, n_tp, n_blk,
    tau_hbm, beta_hbm, tile_hbm, diagrams, loads, out,
    tau, beta, tile, gathered, image, conj_w, w_send, w_recv, image_full,
    partial, shares, blocks,
    load_sem, tile_sem, send_sem, recv_sem, w_send_sem, w_recv_sem,
    share_send_sem, share_recv_sem, block_send_sem, block_recv_sem,
):
    sec, tp, me = lax.axis_index("sec"), lax.axis_index("tp"), lax.axis_index("blk")
    rows, order = tau_hbm.shape[2], tau_hbm.shape[3]
    width = tile_hbm.shape[4]
    half = width // PARTS
    piece = rows // PIECES
    quarter = width // n_blk
    slots = diagrams.shape[1]

    both = jnp.minimum(me, n_blk - 1 - me)
    longer_below = me > n_blk - 1 - me

    def at_step(t):
        in_both = t <= 2 * both
        distance = jnp.where(in_both, lax.div(t + 1, 2), t - both)
        below = jnp.where(in_both, lax.rem(t, 2), jnp.where(longer_below, 1, 0))
        chunk = jnp.where(below == 1, me - distance, me + distance)
        return distance, below, chunk

    def rows_of(chunk):
        return pl.ds(pl.multiple_of(chunk * rows, rows), rows)

    def load(t):
        where = rows_of(at_step(t)[2])
        return (
            pltpu.make_async_copy(
                tau_hbm.at[0, :, :, where], tau.at[:, :, where], load_sem.at[0, t]
            ),
            pltpu.make_async_copy(
                beta_hbm.at[0, :, where, :], beta.at[:, where, :], load_sem.at[1, t]
            ),
        )

    own_tile = pltpu.make_async_copy(tile_hbm.at[0, 0], tile, tile_sem)
    own_tile.start()

    barrier = pltpu.get_barrier_semaphore()
    peers = n_tp * n_blk

    def greet(k, _):
        other_tp, other_blk = lax.div(k, n_blk), lax.rem(k, n_blk)

        @pl.when(jnp.logical_or(other_tp != tp, other_blk != me))
        def _():
            pl.semaphore_signal(
                barrier, inc=1, device_id=(sec, other_tp, other_blk), device_id_type=MESH
            )

        return 0

    lax.fori_loop(0, peers, greet, 0)
    sec_next = lax.rem(sec + 1, n_sec)
    sec_back = lax.rem(sec + n_sec - 1, n_sec)
    greeted = peers - 1
    if n_sec > 1:
        pl.semaphore_signal(barrier, inc=1, device_id=(sec_next, tp, me), device_id_type=MESH)
        greeted += 1
    if n_sec > 2:
        pl.semaphore_signal(barrier, inc=1, device_id=(sec_back, tp, me), device_id_type=MESH)
        greeted += 1

    for t in range(n_blk):
        for copy in load(t):
            copy.start()

    own_tile.wait()
    lane = lax.broadcasted_iota(jnp.int32, (rows, width), 1)
    real = tile[0].astype(jnp.float32)
    imag = tile[1].astype(jnp.float32)
    gathered[0, rows_of(me), :] = jnp.where(
        lane < half, real, pltpu.roll(imag, half, 1)
    ).astype(jnp.bfloat16)
    gathered[1, rows_of(me), :] = jnp.where(
        lane < half, pltpu.roll(real, half, 1), imag
    ).astype(jnp.bfloat16)
    image[...] = jnp.zeros_like(image)
    conj_w[...] = jnp.zeros_like(conj_w)
    pl.semaphore_wait(barrier, greeted)

    def pass_on(upward, distance, part, r):
        chunk = jnp.where(upward == 1, me - distance, me + distance)
        target = jnp.where(upward == 1, me + 1, me - 1)
        where = pl.ds(pl.multiple_of(chunk * rows + r * piece, piece), piece)
        block = gathered.at[part, where, :]
        return pltpu.make_async_remote_copy(
            src_ref=block,
            dst_ref=block,
            send_sem=send_sem.at[upward, distance, part, r],
            recv_sem=recv_sem.at[upward, distance, part, r],
            device_id=(sec, tp, target),
            device_id_type=MESH,
        )

    def arrival(below, distance, part, r):
        chunk = jnp.where(below == 1, me - distance, me + distance)
        where = pl.ds(pl.multiple_of(chunk * rows + r * piece, piece), piece)
        block = gathered.at[part, where, :]
        return pltpu.make_async_remote_copy(
            src_ref=block,
            dst_ref=block,
            send_sem=send_sem.at[below, distance, part, r],
            recv_sem=recv_sem.at[below, distance - 1, part, r],
            device_id=(sec, tp, me),
            device_id_type=MESH,
        )

    def send_own(upward, part):
        for r in range(PIECES):
            pass_on(upward, 0, part, r).start()

    @pl.when(me < n_blk - 1)
    def _():
        send_own(1, 0)

    @pl.when(me > 0)
    def _():
        send_own(0, 0)

    for part in range(1, PARTS):
        @pl.when(me == 0)
        def _():
            send_own(1, part)

        @pl.when(me == n_blk - 1)
        def _():
            send_own(0, part)

    def w_copy(part):
        return pltpu.make_async_remote_copy(
            src_ref=w_send.at[part],
            dst_ref=w_recv.at[part],
            send_sem=w_send_sem.at[part],
            recv_sem=w_recv_sem.at[part],
            device_id=(sec_next, tp, me),
            device_id_type=MESH,
        )

    piece_lane = lax.broadcasted_iota(jnp.int32, (piece, width), 1)
    for part in range(PARTS):
        def step(u, _):
            t, r = lax.div(u, PIECES), lax.rem(u, PIECES)
            distance, below, chunk = at_step(t)

            @pl.when(t > 0)
            def _():
                arrival(below, distance, part, r).wait_recv()
                more = jnp.where(below == 1, me < n_blk - 1, me > 0)

                @pl.when(more)
                def _():
                    pass_on(below, distance, part, r).start()
                    if part + 1 < PARTS:
                        last = jnp.where(below == 1, chunk == 0, chunk == n_blk - 1)

                        @pl.when(jnp.logical_and(last, r == PIECES - 1))
                        def _():
                            send_own(below, part + 1)

            if part == 0:
                @pl.when(r == 0)
                def _():
                    for copy in load(t):
                        copy.wait()

            where = pl.ds(pl.multiple_of(chunk * rows + r * piece, piece), piece)
            straight = gathered[part, where, :]
            wide = straight.astype(jnp.float32)
            turned = pltpu.roll(wide, half, 1)
            turned = jnp.where(piece_lane < half, -turned, turned)
            crossed = turned.astype(jnp.bfloat16)
            image[part] += jnp.dot(
                tau[0, :, where], straight, preferred_element_type=jnp.float32
            ) + jnp.dot(tau[1, :, where], crossed, preferred_element_type=jnp.float32)
            conj_w[part] += jnp.dot(
                wide.T.astype(jnp.bfloat16),
                beta[0, where, :],
                preferred_element_type=jnp.float32,
            ) + jnp.dot(
                (-turned).T.astype(jnp.bfloat16),
                beta[1, where, :],
                preferred_element_type=jnp.float32,
            )
            return 0

        lax.fori_loop(0, n_blk * PIECES, step, 0)
        if n_sec > 1:
            w_send[part] = conj_w[part].astype(jnp.bfloat16)
            w_copy(part).start()
        else:
            w_recv[part] = conj_w[part].astype(jnp.bfloat16)

    first, second = image[0], image[1]
    image_full[:, :width] = jnp.where(
        lane < half, first, pltpu.roll(second, half, 1)
    ).astype(jnp.bfloat16)
    image_full[:, width:] = jnp.where(
        lane < half, pltpu.roll(first, half, 1), second
    ).astype(jnp.bfloat16)

    for part in range(PARTS):
        if n_sec > 1:
            w_copy(part).wait_recv()
        product = jnp.dot(w_recv[part], image_full[...], preferred_element_type=jnp.float32)
        own = pl.ds(part * half, half)
        partial[0, own, :] = (product[:half, :width] + product[half:, width:]).astype(jnp.bfloat16)
        partial[1, own, :] = (product[:half, width:] - product[half:, :width]).astype(jnp.bfloat16)

    def rows_share(q):
        return partial.at[:, pl.ds(pl.multiple_of(q * quarter, quarter), quarter), :]

    def share_copy(distance):
        target = lax.rem(me + distance, n_blk)
        return pltpu.make_async_remote_copy(
            src_ref=rows_share(target),
            dst_ref=shares.at[distance - 1],
            send_sem=share_send_sem.at[distance - 1],
            recv_sem=share_recv_sem.at[distance - 1],
            device_id=(sec, tp, target),
            device_id_type=MESH,
        )

    for distance in range(1, n_blk):
        share_copy(distance).start()
    total = partial[:, pl.ds(pl.multiple_of(me * quarter, quarter), quarter), :].astype(jnp.float32)
    for distance in range(1, n_blk):
        share_copy(distance).wait_recv()
        total = total + shares[distance - 1].astype(jnp.float32)
    blocks[tp, me] = (total * order ** (-0.5)).astype(jnp.bfloat16)

    def block_copy(k, sending):
        other_tp, other_blk = lax.div(k, n_blk), lax.rem(k, n_blk)
        if sending:
            slot, sem = blocks.at[tp, me], block_recv_sem.at[tp, me]
        else:
            slot, sem = blocks.at[other_tp, other_blk], block_recv_sem.at[other_tp, other_blk]
        copy = pltpu.make_async_remote_copy(
            src_ref=slot,
            dst_ref=slot,
            send_sem=block_send_sem.at[other_tp, other_blk],
            recv_sem=sem,
            device_id=(sec, other_tp, other_blk),
            device_id_type=MESH,
        )
        return copy, jnp.logical_or(other_tp != tp, other_blk != me)

    def start_block(k, _):
        copy, other = block_copy(k, True)

        @pl.when(other)
        def _():
            copy.start()

        return 0

    def wait_block(k, _):
        copy, other = block_copy(k, False)

        @pl.when(other)
        def _():
            copy.wait_recv()

        return 0

    lax.fori_loop(0, peers, start_block, 0)
    lax.fori_loop(0, peers, wait_block, 0)

    sums = jnp.zeros((2 * quarter, 2 * width), jnp.float32)
    for g in range(slots):
        active = jnp.where(g < loads[0], 1.0, 0.0)
        left = blocks[diagrams[0, g, 0], me].reshape(2 * quarter, width)
        left = (left.astype(jnp.float32) * active).astype(jnp.bfloat16)
        right = blocks[diagrams[0, g, 1]]
        right = jnp.concatenate(
            [right[:, 0].reshape(width, width), right[:, 1].reshape(width, width)], axis=1
        )
        sums = sums + jnp.dot(left, right, preferred_element_type=jnp.float32)
    scale = (width * slots) ** (-0.5)
    out[0, 0, 0] = (sums[:quarter, :width] - sums[quarter:, width:]) * scale
    out[0, 0, 1] = (sums[:quarter, width:] + sums[quarter:, :width]) * scale

    def drain(u, _):
        distance = lax.div(u, PIECES)
        r = lax.rem(u, PIECES)
        for part in range(PARTS):
            @pl.when(jnp.logical_and(distance <= me, me < n_blk - 1))
            def _():
                pass_on(1, distance, part, r).wait_send()

            @pl.when(jnp.logical_and(me + distance < n_blk, me > 0))
            def _():
                pass_on(0, distance, part, r).wait_send()

        return 0

    lax.fori_loop(0, n_blk * PIECES, drain, 0)
    if n_sec > 1:
        for part in range(PARTS):
            w_copy(part).wait_send()
    for distance in range(1, n_blk):
        share_copy(distance).wait_send()

    def drain_block(k, _):
        copy, other = block_copy(k, True)

        @pl.when(other)
        def _():
            copy.wait_send()

        return 0

    lax.fori_loop(0, peers, drain_block, 0)


def on_device(n_sec, n_tp, n_blk, perambulator, backward, elementals, diagrams, owner_loads):
    rows, order = perambulator.shape[2:]
    width = elementals.shape[4]
    half = width // PARTS
    quarter = width // n_blk
    any_space = pl.BlockSpec(memory_space=pl.ANY)
    smem = pl.BlockSpec(memory_space=pltpu.SMEM)
    dma = pltpu.SemaphoreType.DMA
    return pl.pallas_call(
        functools.partial(kernel, n_sec, n_tp, n_blk),
        out_shape=jax.ShapeDtypeStruct((1, 1, 2, quarter, width), jnp.float32),
        in_specs=[any_space, any_space, any_space, smem, smem],
        out_specs=pl.BlockSpec(memory_space=pltpu.VMEM),
        scratch_shapes=[
            pltpu.VMEM((2, rows, order), jnp.bfloat16),
            pltpu.VMEM((2, order, rows), jnp.bfloat16),
            pltpu.VMEM((2, rows, width), jnp.bfloat16),
            pltpu.VMEM((PARTS, order, 2 * half), jnp.bfloat16),
            pltpu.VMEM((PARTS, rows, 2 * half), jnp.float32),
            pltpu.VMEM((PARTS, 2 * half, rows), jnp.float32),
            pltpu.VMEM((PARTS, 2 * half, rows), jnp.bfloat16),
            pltpu.VMEM((PARTS, 2 * half, rows), jnp.bfloat16),
            pltpu.VMEM((rows, 2 * width), jnp.bfloat16),
            pltpu.VMEM((2, width, width), jnp.bfloat16),
            pltpu.VMEM((n_blk, 2, quarter, width), jnp.bfloat16),
            pltpu.VMEM((n_tp, n_blk, 2, quarter, width), jnp.bfloat16),
            dma((2, n_blk)),
            dma,
            dma((2, n_blk, PARTS, PIECES)),
            dma((2, n_blk, PARTS, PIECES)),
            dma((PARTS,)),
            dma((PARTS,)),
            dma((n_blk,)),
            dma((n_blk,)),
            dma((n_tp, n_blk)),
            dma((n_tp, n_blk)),
        ],
        compiler_params=pltpu.CompilerParams(
            collective_id=0, has_side_effects=True, vmem_limit_bytes=40 * 1024 * 1024
        ),
    )(perambulator, backward, elementals, diagrams, owner_loads)


def solution(mesh):
    placed = (
        P("tp", None, "blk", None),
        P("tp", None, None, "blk"),
        P("sec", "tp", None, "blk", None),
        P("tp", None, None),
        P("tp"),
    )
    sizes = (mesh.shape["sec"], mesh.shape["tp"], mesh.shape["blk"])
    return jax.shard_map(
        functools.partial(on_device, *sizes),
        mesh=mesh,
        in_specs=placed,
        out_specs=P("sec", "tp", None, "blk", None),
        check_vma=False,
    )
```

```python
import functools

import jax
import jax.numpy as jnp
from jax import lax
from jax.experimental import pallas as pl
from jax.experimental.pallas import tpu as pltpu
from jax.sharding import PartitionSpec as P

PARTS = 2
PIECES = 2
MESH = pl.DeviceIdType.MESH


def kernel(
    n_sec, n_tp, n_blk,
    tau_hbm, beta_hbm, tile_hbm, diagrams, loads, out,
    tau, beta, tile, gathered, image, conj_w, w_send, w_recv, image_full,
    partial, shares, blocks,
    load_sem, tile_sem, send_sem, recv_sem, w_send_sem, w_recv_sem,
    share_send_sem, share_recv_sem, block_send_sem, block_recv_sem,
):
    sec, tp, me = lax.axis_index("sec"), lax.axis_index("tp"), lax.axis_index("blk")
    rows, order = tau_hbm.shape[2], tau_hbm.shape[3]
    width = tile_hbm.shape[4]
    half = width // PARTS
    piece = rows // PIECES
    quarter = width // n_blk
    slots = diagrams.shape[2]

    both = jnp.minimum(me, n_blk - 1 - me)
    longer_below = me > n_blk - 1 - me

    def at_step(t):
        in_both = t <= 2 * both
        distance = jnp.where(in_both, lax.div(t + 1, 2), t - both)
        below = jnp.where(in_both, lax.rem(t, 2), jnp.where(longer_below, 1, 0))
        chunk = jnp.where(below == 1, me - distance, me + distance)
        return distance, below, chunk

    def rows_of(chunk):
        return pl.ds(pl.multiple_of(chunk * rows, rows), rows)

    def load(t):
        where = rows_of(at_step(t)[2])
        return (
            pltpu.make_async_copy(
                tau_hbm.at[0, :, :, where], tau.at[:, :, where], load_sem.at[0, t]
            ),
            pltpu.make_async_copy(
                beta_hbm.at[0, :, where, :], beta.at[:, where, :], load_sem.at[1, t]
            ),
        )

    own_tile = pltpu.make_async_copy(tile_hbm.at[0, 0], tile, tile_sem)
    own_tile.start()

    barrier = pltpu.get_barrier_semaphore()
    peers = n_tp * n_blk

    def greet(k, _):
        other_tp, other_blk = lax.div(k, n_blk), lax.rem(k, n_blk)

        @pl.when(jnp.logical_or(other_tp != tp, other_blk != me))
        def _():
            pl.semaphore_signal(
                barrier, inc=1, device_id=(sec, other_tp, other_blk), device_id_type=MESH
            )

        return 0

    lax.fori_loop(0, peers, greet, 0)
    sec_next = lax.rem(sec + 1, n_sec)
    sec_back = lax.rem(sec + n_sec - 1, n_sec)
    greeted = peers - 1
    if n_sec > 1:
        pl.semaphore_signal(barrier, inc=1, device_id=(sec_next, tp, me), device_id_type=MESH)
        greeted += 1
    if n_sec > 2:
        pl.semaphore_signal(barrier, inc=1, device_id=(sec_back, tp, me), device_id_type=MESH)
        greeted += 1

    for t in range(n_blk):
        for copy in load(t):
            copy.start()

    own_tile.wait()
    lane = lax.broadcasted_iota(jnp.int32, (rows, width), 1)
    real = tile[0].astype(jnp.float32)
    imag = tile[1].astype(jnp.float32)
    gathered[0, rows_of(me), :] = jnp.where(
        lane < half, real, pltpu.roll(imag, half, 1)
    ).astype(jnp.bfloat16)
    gathered[1, rows_of(me), :] = jnp.where(
        lane < half, pltpu.roll(real, half, 1), imag
    ).astype(jnp.bfloat16)
    image[...] = jnp.zeros_like(image)
    conj_w[...] = jnp.zeros_like(conj_w)
    pl.semaphore_wait(barrier, greeted)

    def pass_on(upward, distance, part, r):
        chunk = jnp.where(upward == 1, me - distance, me + distance)
        target = jnp.where(upward == 1, me + 1, me - 1)
        where = pl.ds(pl.multiple_of(chunk * rows + r * piece, piece), piece)
        block = gathered.at[part, where, :]
        return pltpu.make_async_remote_copy(
            src_ref=block,
            dst_ref=block,
            send_sem=send_sem.at[upward, distance, part, r],
            recv_sem=recv_sem.at[upward, distance, part, r],
            device_id=(sec, tp, target),
            device_id_type=MESH,
        )

    def arrival(below, distance, part, r):
        chunk = jnp.where(below == 1, me - distance, me + distance)
        where = pl.ds(pl.multiple_of(chunk * rows + r * piece, piece), piece)
        block = gathered.at[part, where, :]
        return pltpu.make_async_remote_copy(
            src_ref=block,
            dst_ref=block,
            send_sem=send_sem.at[below, distance, part, r],
            recv_sem=recv_sem.at[below, distance - 1, part, r],
            device_id=(sec, tp, me),
            device_id_type=MESH,
        )

    def send_own(upward, part):
        for r in range(PIECES):
            pass_on(upward, 0, part, r).start()

    @pl.when(me < n_blk - 1)
    def _():
        send_own(1, 0)

    @pl.when(me > 0)
    def _():
        send_own(0, 0)

    for part in range(1, PARTS):
        @pl.when(me == 0)
        def _():
            send_own(1, part)

        @pl.when(me == n_blk - 1)
        def _():
            send_own(0, part)

    def w_copy(part):
        return pltpu.make_async_remote_copy(
            src_ref=w_send.at[part],
            dst_ref=w_recv.at[part],
            send_sem=w_send_sem.at[part],
            recv_sem=w_recv_sem.at[part],
            device_id=(sec_next, tp, me),
            device_id_type=MESH,
        )

    piece_lane = lax.broadcasted_iota(jnp.int32, (piece, width), 1)
    for part in range(PARTS):
        def step(u, _):
            t, r = lax.div(u, PIECES), lax.rem(u, PIECES)
            distance, below, chunk = at_step(t)

            @pl.when(t > 0)
            def _():
                arrival(below, distance, part, r).wait_recv()
                more = jnp.where(below == 1, me < n_blk - 1, me > 0)

                @pl.when(more)
                def _():
                    pass_on(below, distance, part, r).start()
                    if part + 1 < PARTS:
                        last = jnp.where(below == 1, chunk == 0, chunk == n_blk - 1)

                        @pl.when(jnp.logical_and(last, r == PIECES - 1))
                        def _():
                            send_own(below, part + 1)

            if part == 0:
                @pl.when(r == 0)
                def _():
                    for copy in load(t):
                        copy.wait()

            where = pl.ds(pl.multiple_of(chunk * rows + r * piece, piece), piece)
            straight = gathered[part, where, :]
            wide = straight.astype(jnp.float32)
            turned = pltpu.roll(wide, half, 1)
            turned = jnp.where(piece_lane < half, -turned, turned)
            crossed = turned.astype(jnp.bfloat16)
            image[part] += jnp.dot(
                tau[0, :, where], straight, preferred_element_type=jnp.float32
            ) + jnp.dot(tau[1, :, where], crossed, preferred_element_type=jnp.float32)
            conj_w[part] += jnp.dot(
                wide.T.astype(jnp.bfloat16),
                beta[0, where, :],
                preferred_element_type=jnp.float32,
            ) + jnp.dot(
                (-turned).T.astype(jnp.bfloat16),
                beta[1, where, :],
                preferred_element_type=jnp.float32,
            )
            return 0

        lax.fori_loop(0, n_blk * PIECES, step, 0)
        if n_sec > 1:
            w_send[part] = conj_w[part].astype(jnp.bfloat16)
            w_copy(part).start()
        else:
            w_recv[part] = conj_w[part].astype(jnp.bfloat16)

    first, second = image[0], image[1]
    image_full[:, :width] = jnp.where(
        lane < half, first, pltpu.roll(second, half, 1)
    ).astype(jnp.bfloat16)
    image_full[:, width:] = jnp.where(
        lane < half, pltpu.roll(first, half, 1), second
    ).astype(jnp.bfloat16)

    for part in range(PARTS):
        if n_sec > 1:
            w_copy(part).wait_recv()
        product = jnp.dot(w_recv[part], image_full[...], preferred_element_type=jnp.float32)
        own = pl.ds(part * half, half)
        partial[0, own, :] = (product[:half, :width] + product[half:, width:]).astype(jnp.bfloat16)
        partial[1, own, :] = (product[:half, width:] - product[half:, :width]).astype(jnp.bfloat16)

    def rows_share(q):
        return partial.at[:, pl.ds(pl.multiple_of(q * quarter, quarter), quarter), :]

    def share_copy(distance):
        target = lax.rem(me + distance, n_blk)
        return pltpu.make_async_remote_copy(
            src_ref=rows_share(target),
            dst_ref=shares.at[distance - 1],
            send_sem=share_send_sem.at[distance - 1],
            recv_sem=share_recv_sem.at[distance - 1],
            device_id=(sec, tp, target),
            device_id_type=MESH,
        )

    for distance in range(1, n_blk):
        share_copy(distance).start()
    total = partial[:, pl.ds(pl.multiple_of(me * quarter, quarter), quarter), :].astype(jnp.float32)
    for distance in range(1, n_blk):
        share_copy(distance).wait_recv()
        total = total + shares[distance - 1].astype(jnp.float32)
    blocks[tp, me] = (total * order ** (-0.5)).astype(jnp.bfloat16)

    def block_copy(k, sending):
        other_tp, other_blk = lax.div(k, n_blk), lax.rem(k, n_blk)
        if sending:
            slot, sem = blocks.at[tp, me], block_recv_sem.at[tp, me]
        else:
            slot, sem = blocks.at[other_tp, other_blk], block_recv_sem.at[other_tp, other_blk]
        copy = pltpu.make_async_remote_copy(
            src_ref=slot,
            dst_ref=slot,
            send_sem=block_send_sem.at[other_tp, other_blk],
            recv_sem=sem,
            device_id=(sec, other_tp, other_blk),
            device_id_type=MESH,
        )
        return copy, jnp.logical_or(other_tp != tp, other_blk != me)

    def start_block(k, _):
        copy, other = block_copy(k, True)

        @pl.when(other)
        def _():
            copy.start()

        return 0

    def wait_block(k, _):
        copy, other = block_copy(k, False)

        @pl.when(other)
        def _():
            copy.wait_recv()

        return 0

    lax.fori_loop(0, peers, start_block, 0)
    lax.fori_loop(0, peers, wait_block, 0)

    sums = jnp.zeros((2 * quarter, 2 * width), jnp.float32)
    for g in range(slots):
        active = jnp.where(g < loads[0], 1.0, 0.0)
        left = blocks[diagrams[0, 0, g], me].reshape(2 * quarter, width)
        left = (left.astype(jnp.float32) * active).astype(jnp.bfloat16)
        right = blocks[diagrams[0, 1, g]]
        right = jnp.concatenate(
            [right[:, 0].reshape(width, width), right[:, 1].reshape(width, width)], axis=1
        )
        sums = sums + jnp.dot(left, right, preferred_element_type=jnp.float32)
    scale = (width * slots) ** (-0.5)
    out[0, 0, 0] = (sums[:quarter, :width] - sums[quarter:, width:]) * scale
    out[0, 0, 1] = (sums[:quarter, width:] + sums[quarter:, :width]) * scale

    def drain(u, _):
        distance = lax.div(u, PIECES)
        r = lax.rem(u, PIECES)
        for part in range(PARTS):
            @pl.when(jnp.logical_and(distance <= me, me < n_blk - 1))
            def _():
                pass_on(1, distance, part, r).wait_send()

            @pl.when(jnp.logical_and(me + distance < n_blk, me > 0))
            def _():
                pass_on(0, distance, part, r).wait_send()

        return 0

    lax.fori_loop(0, n_blk * PIECES, drain, 0)
    if n_sec > 1:
        for part in range(PARTS):
            w_copy(part).wait_send()
    for distance in range(1, n_blk):
        share_copy(distance).wait_send()

    def drain_block(k, _):
        copy, other = block_copy(k, True)

        @pl.when(other)
        def _():
            copy.wait_send()

        return 0

    lax.fori_loop(0, peers, drain_block, 0)


def on_device(n_sec, n_tp, n_blk, perambulator, backward, elementals, diagrams, owner_loads):
    rows, order = perambulator.shape[2:]
    width = elementals.shape[4]
    half = width // PARTS
    quarter = width // n_blk
    hbm = pl.BlockSpec(memory_space=pltpu.HBM)
    smem = pl.BlockSpec(memory_space=pltpu.SMEM)
    dma = pltpu.SemaphoreType.DMA
    return pl.pallas_call(
        functools.partial(kernel, n_sec, n_tp, n_blk),
        out_shape=jax.ShapeDtypeStruct((1, 1, 2, quarter, width), jnp.float32),
        in_specs=[hbm, hbm, hbm, smem, smem],
        out_specs=pl.BlockSpec(memory_space=pltpu.VMEM),
        scratch_shapes=[
            pltpu.VMEM((2, rows, order), jnp.bfloat16),
            pltpu.VMEM((2, order, rows), jnp.bfloat16),
            pltpu.VMEM((2, rows, width), jnp.bfloat16),
            pltpu.VMEM((PARTS, order, 2 * half), jnp.bfloat16),
            pltpu.VMEM((PARTS, rows, 2 * half), jnp.float32),
            pltpu.VMEM((PARTS, 2 * half, rows), jnp.float32),
            pltpu.VMEM((PARTS, 2 * half, rows), jnp.bfloat16),
            pltpu.VMEM((PARTS, 2 * half, rows), jnp.bfloat16),
            pltpu.VMEM((rows, 2 * width), jnp.bfloat16),
            pltpu.VMEM((2, width, width), jnp.bfloat16),
            pltpu.VMEM((n_blk, 2, quarter, width), jnp.bfloat16),
            pltpu.VMEM((n_tp, n_blk, 2, quarter, width), jnp.bfloat16),
            dma((2, n_blk)),
            dma,
            dma((2, n_blk, PARTS, PIECES)),
            dma((2, n_blk, PARTS, PIECES)),
            dma((PARTS,)),
            dma((PARTS,)),
            dma((n_blk,)),
            dma((n_blk,)),
            dma((n_tp, n_blk)),
            dma((n_tp, n_blk)),
        ],
        compiler_params=pltpu.CompilerParams(
            collective_id=0, has_side_effects=True, vmem_limit_bytes=40 * 1024 * 1024
        ),
    )(perambulator, backward, elementals, jnp.swapaxes(diagrams, 1, 2), owner_loads)


def solution(mesh):
    placed = (
        P("tp", None, "blk", None),
        P("tp", None, None, "blk"),
        P("sec", "tp", None, "blk", None),
        P("tp", None, None),
        P("tp"),
    )
    sizes = (mesh.shape["sec"], mesh.shape["tp"], mesh.shape["blk"])
    return jax.shard_map(
        functools.partial(on_device, *sizes),
        mesh=mesh,
        in_specs=placed,
        out_specs=P("sec", "tp", None, "blk", None),
        check_vma=False,
    )
```

```python
import functools

import jax
import jax.numpy as jnp
from jax import lax
from jax.experimental import pallas as pl
from jax.experimental.pallas import tpu as pltpu
from jax.sharding import PartitionSpec as P

PARTS = 2
PIECES = 2
MESH = pl.DeviceIdType.MESH


def kernel(
    n_sec, n_tp, n_blk,
    tau_hbm, beta_hbm, tile_hbm, diagrams, loads, out,
    tau, beta, tile, gathered, image, conj_w, w_send, w_recv, image_full,
    partial, shares, blocks,
    load_sem, tile_sem, send_sem, recv_sem, w_send_sem, w_recv_sem,
    share_send_sem, share_recv_sem, block_send_sem, block_recv_sem, pair_send_sem,
):
    sec, tp, me = lax.axis_index("sec"), lax.axis_index("tp"), lax.axis_index("blk")
    rows, order = tau_hbm.shape[2], tau_hbm.shape[3]
    width = tile_hbm.shape[4]
    half = width // PARTS
    piece = rows // PIECES
    quarter = width // n_blk
    slots = diagrams.shape[2]

    both = jnp.minimum(me, n_blk - 1 - me)
    longer_below = me > n_blk - 1 - me

    def at_step(t):
        in_both = t <= 2 * both
        distance = jnp.where(in_both, lax.div(t + 1, 2), t - both)
        below = jnp.where(in_both, lax.rem(t, 2), jnp.where(longer_below, 1, 0))
        chunk = jnp.where(below == 1, me - distance, me + distance)
        return distance, below, chunk

    def rows_of(chunk):
        return pl.ds(pl.multiple_of(chunk * rows, rows), rows)

    def load(t):
        where = rows_of(at_step(t)[2])
        return (
            pltpu.make_async_copy(
                tau_hbm.at[0, :, :, where], tau.at[:, :, where], load_sem.at[0, t]
            ),
            pltpu.make_async_copy(
                beta_hbm.at[0, :, where, :], beta.at[:, where, :], load_sem.at[1, t]
            ),
        )

    own_tile = pltpu.make_async_copy(tile_hbm.at[0, 0], tile, tile_sem)
    own_tile.start()

    barrier = pltpu.get_barrier_semaphore()
    peers = n_tp * n_blk

    cores = 2 if n_tp % 2 == 0 else 1
    core = lax.rem(tp, cores)
    sibling = tp + 1 - 2 * core

    def same_core(other_tp, other_blk):
        other = jnp.logical_or(other_tp != tp, other_blk != me)
        return jnp.logical_and(other, lax.rem(other_tp, cores) == core)

    def greet(k, _):
        other_tp, other_blk = lax.div(k, n_blk), lax.rem(k, n_blk)

        @pl.when(same_core(other_tp, other_blk))
        def _():
            pl.semaphore_signal(
                barrier, inc=1, device_id=(sec, other_tp, other_blk), device_id_type=MESH
            )

        return 0

    lax.fori_loop(0, peers, greet, 0)
    sec_next = lax.rem(sec + 1, n_sec)
    sec_back = lax.rem(sec + n_sec - 1, n_sec)
    greeted = peers // cores - 1
    if cores > 1:
        pl.semaphore_signal(barrier, inc=1, device_id=(sec, sibling, me), device_id_type=MESH)
        greeted += 1
    if n_sec > 1:
        pl.semaphore_signal(barrier, inc=1, device_id=(sec_next, tp, me), device_id_type=MESH)
        greeted += 1
    if n_sec > 2:
        pl.semaphore_signal(barrier, inc=1, device_id=(sec_back, tp, me), device_id_type=MESH)
        greeted += 1

    for t in range(n_blk):
        for copy in load(t):
            copy.start()

    own_tile.wait()
    lane = lax.broadcasted_iota(jnp.int32, (rows, width), 1)
    real = tile[0].astype(jnp.float32)
    imag = tile[1].astype(jnp.float32)
    gathered[0, rows_of(me), :] = jnp.where(
        lane < half, real, pltpu.roll(imag, half, 1)
    ).astype(jnp.bfloat16)
    gathered[1, rows_of(me), :] = jnp.where(
        lane < half, pltpu.roll(real, half, 1), imag
    ).astype(jnp.bfloat16)
    image[...] = jnp.zeros_like(image)
    dense = n_tp * n_tp <= slots
    if dense:
        counts = [[jnp.float32(0)] * n_tp for _ in range(n_tp)]
        for g in range(slots):
            left, right = diagrams[0, 0, g], diagrams[0, 1, g]
            live = g < loads[0]
            for a in range(n_tp):
                in_a = jnp.where(jnp.logical_and(live, left == a), 1.0, 0.0)
                for b in range(n_tp):
                    counts[a][b] = counts[a][b] + jnp.where(right == b, in_a, 0.0)
    conj_w[...] = jnp.zeros_like(conj_w)
    pl.semaphore_wait(barrier, greeted)

    def pass_on(upward, distance, part, r):
        chunk = jnp.where(upward == 1, me - distance, me + distance)
        target = jnp.where(upward == 1, me + 1, me - 1)
        where = pl.ds(pl.multiple_of(chunk * rows + r * piece, piece), piece)
        block = gathered.at[part, where, :]
        return pltpu.make_async_remote_copy(
            src_ref=block,
            dst_ref=block,
            send_sem=send_sem.at[upward, distance, part, r],
            recv_sem=recv_sem.at[upward, distance, part, r],
            device_id=(sec, tp, target),
            device_id_type=MESH,
        )

    def arrival(below, distance, part, r):
        chunk = jnp.where(below == 1, me - distance, me + distance)
        where = pl.ds(pl.multiple_of(chunk * rows + r * piece, piece), piece)
        block = gathered.at[part, where, :]
        return pltpu.make_async_remote_copy(
            src_ref=block,
            dst_ref=block,
            send_sem=send_sem.at[below, distance, part, r],
            recv_sem=recv_sem.at[below, distance - 1, part, r],
            device_id=(sec, tp, me),
            device_id_type=MESH,
        )

    def send_own(upward, part):
        for r in range(PIECES):
            pass_on(upward, 0, part, r).start()

    @pl.when(me < n_blk - 1)
    def _():
        send_own(1, 0)

    @pl.when(me > 0)
    def _():
        send_own(0, 0)

    for part in range(1, PARTS):
        @pl.when(me == 0)
        def _():
            send_own(1, part)

        @pl.when(me == n_blk - 1)
        def _():
            send_own(0, part)

    def w_copy(part):
        return pltpu.make_async_remote_copy(
            src_ref=w_send.at[part],
            dst_ref=w_recv.at[part],
            send_sem=w_send_sem.at[part],
            recv_sem=w_recv_sem.at[part],
            device_id=(sec_next, tp, me),
            device_id_type=MESH,
        )

    piece_lane = lax.broadcasted_iota(jnp.int32, (piece, width), 1)
    for part in range(PARTS):
        def receive(u):
            t, r = lax.div(u, PIECES), lax.rem(u, PIECES)
            distance, below, chunk = at_step(t)

            @pl.when(jnp.logical_and(t > 0, u < n_blk * PIECES))
            def _():
                arrival(below, distance, part, r).wait_recv()
                more = jnp.where(below == 1, me < n_blk - 1, me > 0)

                @pl.when(more)
                def _():
                    pass_on(below, distance, part, r).start()
                    if part + 1 < PARTS:
                        last = jnp.where(below == 1, chunk == 0, chunk == n_blk - 1)

                        @pl.when(jnp.logical_and(last, r == PIECES - 1))
                        def _():
                            send_own(below, part + 1)

        def step(u, _):
            t, r = lax.div(u, PIECES), lax.rem(u, PIECES)
            chunk = at_step(t)[2]

            @pl.when(both > 0)
            def _():
                receive(u + 1)

            if part == 0:
                @pl.when(r == 0)
                def _():
                    for copy in load(t):
                        copy.wait()

            where = pl.ds(pl.multiple_of(chunk * rows + r * piece, piece), piece)
            straight = gathered[part, where, :]
            wide = straight.astype(jnp.float32)
            turned = pltpu.roll(wide, half, 1)
            turned = jnp.where(piece_lane < half, -turned, turned)
            crossed = turned.astype(jnp.bfloat16)
            image[part] += jnp.dot(
                tau[0, :, where], straight, preferred_element_type=jnp.float32
            ) + jnp.dot(tau[1, :, where], crossed, preferred_element_type=jnp.float32)
            conj_w[part] += jnp.dot(
                wide.T.astype(jnp.bfloat16),
                beta[0, where, :],
                preferred_element_type=jnp.float32,
            ) + jnp.dot(
                (-turned).T.astype(jnp.bfloat16),
                beta[1, where, :],
                preferred_element_type=jnp.float32,
            )

            @pl.when(both == 0)
            def _():
                receive(u + 1)

            return 0

        lax.fori_loop(0, n_blk * PIECES, step, 0)
        if n_sec > 1:
            w_send[part] = conj_w[part].astype(jnp.bfloat16)
            w_copy(part).start()
        else:
            w_recv[part] = conj_w[part].astype(jnp.bfloat16)

    first, second = image[0], image[1]
    image_full[:, :width] = jnp.where(
        lane < half, first, pltpu.roll(second, half, 1)
    ).astype(jnp.bfloat16)
    image_full[:, width:] = jnp.where(
        lane < half, pltpu.roll(first, half, 1), second
    ).astype(jnp.bfloat16)

    for part in range(PARTS):
        if n_sec > 1:
            w_copy(part).wait_recv()
        product = jnp.dot(w_recv[part], image_full[...], preferred_element_type=jnp.float32)
        own = pl.ds(part * half, half)
        partial[0, own, :] = (product[:half, :width] + product[half:, width:]).astype(jnp.bfloat16)
        partial[1, own, :] = (product[:half, width:] - product[half:, :width]).astype(jnp.bfloat16)

    def rows_share(q):
        return partial.at[:, pl.ds(pl.multiple_of(q * quarter, quarter), quarter), :]

    def share_copy(distance):
        target = lax.rem(me + distance, n_blk)
        return pltpu.make_async_remote_copy(
            src_ref=rows_share(target),
            dst_ref=shares.at[distance - 1],
            send_sem=share_send_sem.at[distance - 1],
            recv_sem=share_recv_sem.at[distance - 1],
            device_id=(sec, tp, target),
            device_id_type=MESH,
        )

    for distance in range(1, n_blk):
        share_copy(distance).start()

    def drain(u, _):
        distance = lax.div(u, PIECES)
        r = lax.rem(u, PIECES)
        for part in range(PARTS):
            @pl.when(jnp.logical_and(distance <= me, me < n_blk - 1))
            def _():
                pass_on(1, distance, part, r).wait_send()

            @pl.when(jnp.logical_and(me + distance < n_blk, me > 0))
            def _():
                pass_on(0, distance, part, r).wait_send()

        return 0

    lax.fori_loop(0, n_blk * PIECES, drain, 0)
    total = partial[:, pl.ds(pl.multiple_of(me * quarter, quarter), quarter), :].astype(jnp.float32)
    for distance in range(1, n_blk):
        share_copy(distance).wait_recv()
        total = total + shares[distance - 1].astype(jnp.float32)
    blocks[tp, me] = (total * order ** (-0.5)).astype(jnp.bfloat16)

    def block_copy(from_tp, from_blk, to_tp, to_blk, sem):
        slot = blocks.at[from_tp, from_blk]
        return pltpu.make_async_remote_copy(
            src_ref=slot,
            dst_ref=slot,
            send_sem=sem,
            recv_sem=block_recv_sem.at[from_tp, from_blk],
            device_id=(sec, to_tp, to_blk),
            device_id_type=MESH,
        )

    def own_block(k):
        other_tp, other_blk = lax.div(k, n_blk), lax.rem(k, n_blk)
        copy = block_copy(tp, me, other_tp, other_blk, block_send_sem.at[other_tp, other_blk])
        return copy, same_core(other_tp, other_blk)

    def sibling_block(k):
        from_tp, from_blk = lax.div(k, n_blk), lax.rem(k, n_blk)
        copy = block_copy(from_tp, from_blk, sibling, me, pair_send_sem.at[from_tp, from_blk])
        return copy, lax.rem(from_tp, cores) == core

    def start_block(k, _):
        copy, wanted = own_block(k)

        @pl.when(wanted)
        def _():
            copy.start()

        return 0

    def wait_block(k, _):
        other_tp, other_blk = lax.div(k, n_blk), lax.rem(k, n_blk)

        @pl.when(same_core(other_tp, other_blk))
        def _():
            block_copy(
                other_tp, other_blk, tp, me, block_send_sem.at[other_tp, other_blk]
            ).wait_recv()
            if cores > 1:
                sibling_block(k)[0].start()

        return 0

    def wait_pair(k, _):
        copy, passed = sibling_block(k)

        @pl.when(jnp.logical_not(passed))
        def _():
            copy.wait_recv()

        return 0

    lax.fori_loop(0, peers, start_block, 0)
    if cores > 1:
        block_copy(tp, me, sibling, me, pair_send_sem.at[tp, me]).start()
    if n_sec > 1:
        for part in range(PARTS):
            w_copy(part).wait_send()
    for distance in range(1, n_blk):
        share_copy(distance).wait_send()
    lax.fori_loop(0, peers, wait_block, 0)
    if cores > 1:
        lax.fori_loop(0, peers, wait_pair, 0)

    def right_of(index):
        right = blocks[index]
        return jnp.concatenate(
            [right[:, 0].reshape(width, width), right[:, 1].reshape(width, width)], axis=1
        )

    if dense:
        lefts = [blocks[a, me].reshape(2 * quarter, width).astype(jnp.float32) for a in range(n_tp)]
        sums = jnp.zeros((4 * quarter, 2 * width), jnp.float32)
        for b in range(n_tp):
            left = lefts[0] * counts[0][b]
            for a in range(1, n_tp):
                left = left + lefts[a] * counts[a][b]
            high = left.astype(jnp.bfloat16)
            low = (left - high.astype(jnp.float32)).astype(jnp.bfloat16)
            sums = sums + jnp.dot(
                jnp.concatenate([high, low], axis=0),
                right_of(b),
                preferred_element_type=jnp.float32,
            )
        sums = sums[: 2 * quarter] + sums[2 * quarter :]
    else:
        sums = jnp.zeros((2 * quarter, 2 * width), jnp.float32)
        for g in range(slots):
            active = jnp.where(g < loads[0], 1.0, 0.0)
            left = blocks[diagrams[0, 0, g], me].reshape(2 * quarter, width)
            left = (left.astype(jnp.float32) * active).astype(jnp.bfloat16)
            sums = sums + jnp.dot(
                left, right_of(diagrams[0, 1, g]), preferred_element_type=jnp.float32
            )
    scale = (width * slots) ** (-0.5)
    out[0, 0, 0] = (sums[:quarter, :width] - sums[quarter:, width:]) * scale
    out[0, 0, 1] = (sums[:quarter, width:] + sums[quarter:, :width]) * scale


    def drain_block(k, _):
        copy, sent = own_block(k)

        @pl.when(sent)
        def _():
            copy.wait_send()

        if cores > 1:
            pair_copy, passed = sibling_block(k)

            @pl.when(passed)
            def _():
                pair_copy.wait_send()

        return 0

    lax.fori_loop(0, peers, drain_block, 0)


def on_device(n_sec, n_tp, n_blk, perambulator, backward, elementals, diagrams, owner_loads):
    rows, order = perambulator.shape[2:]
    width = elementals.shape[4]
    half = width // PARTS
    quarter = width // n_blk
    hbm = pl.BlockSpec(memory_space=pltpu.HBM)
    smem = pl.BlockSpec(memory_space=pltpu.SMEM)
    dma = pltpu.SemaphoreType.DMA
    return pl.pallas_call(
        functools.partial(kernel, n_sec, n_tp, n_blk),
        out_shape=jax.ShapeDtypeStruct((1, 1, 2, quarter, width), jnp.float32),
        in_specs=[hbm, hbm, hbm, smem, smem],
        out_specs=pl.BlockSpec(memory_space=pltpu.VMEM),
        scratch_shapes=[
            pltpu.VMEM((2, rows, order), jnp.bfloat16),
            pltpu.VMEM((2, order, rows), jnp.bfloat16),
            pltpu.VMEM((2, rows, width), jnp.bfloat16),
            pltpu.VMEM((PARTS, order, 2 * half), jnp.bfloat16),
            pltpu.VMEM((PARTS, rows, 2 * half), jnp.float32),
            pltpu.VMEM((PARTS, 2 * half, rows), jnp.float32),
            pltpu.VMEM((PARTS, 2 * half, rows), jnp.bfloat16),
            pltpu.VMEM((PARTS, 2 * half, rows), jnp.bfloat16),
            pltpu.VMEM((rows, 2 * width), jnp.bfloat16),
            pltpu.VMEM((2, width, width), jnp.bfloat16),
            pltpu.VMEM((n_blk, 2, quarter, width), jnp.bfloat16),
            pltpu.VMEM((n_tp, n_blk, 2, quarter, width), jnp.bfloat16),
            dma((2, n_blk)),
            dma,
            dma((2, n_blk, PARTS, PIECES)),
            dma((2, n_blk, PARTS, PIECES)),
            dma((PARTS,)),
            dma((PARTS,)),
            dma((n_blk,)),
            dma((n_blk,)),
            dma((n_tp, n_blk)),
            dma((n_tp, n_blk)),
            dma((n_tp, n_blk)),
        ],
        compiler_params=pltpu.CompilerParams(
            collective_id=0, has_side_effects=True, vmem_limit_bytes=60 * 1024 * 1024
        ),
    )(perambulator, backward, elementals, jnp.swapaxes(diagrams, 1, 2), owner_loads)


def solution(mesh):
    placed = (
        P("tp", None, "blk", None),
        P("tp", None, None, "blk"),
        P("sec", "tp", None, "blk", None),
        P("tp", None, None),
        P("tp"),
    )
    sizes = (mesh.shape["sec"], mesh.shape["tp"], mesh.shape["blk"])
    return jax.shard_map(
        functools.partial(on_device, *sizes),
        mesh=mesh,
        in_specs=placed,
        out_specs=P("sec", "tp", None, "blk", None),
        check_vma=False,
    )
```

```python
import functools

import jax
import jax.numpy as jnp
from jax import lax
from jax.experimental import pallas as pl
from jax.experimental.pallas import tpu as pltpu
from jax.sharding import PartitionSpec as P

PARTS = 2
PIECES = 2
MESH = pl.DeviceIdType.MESH


def kernel(
    n_sec, n_tp, n_blk,
    tau_hbm, beta_hbm, tile_hbm, diagrams, loads, out,
    tau, beta, tile, gathered, image, conj_w, w_send, w_recv, image_full,
    partial, shares, blocks,
    load_sem, tile_sem, send_sem, recv_sem, w_send_sem, w_recv_sem,
    share_send_sem, share_recv_sem, block_send_sem, block_recv_sem, pair_send_sem,
):
    sec, tp, me = lax.axis_index("sec"), lax.axis_index("tp"), lax.axis_index("blk")
    rows, order = tau_hbm.shape[2], tau_hbm.shape[3]
    width = tile_hbm.shape[4]
    half = width // PARTS
    piece = rows // PIECES
    quarter = width // n_blk
    slots = diagrams.shape[2]

    both = jnp.minimum(me, n_blk - 1 - me)
    longer_below = me > n_blk - 1 - me

    def at_step(t):
        in_both = t <= 2 * both
        distance = jnp.where(in_both, lax.div(t + 1, 2), t - both)
        below = jnp.where(in_both, lax.rem(t, 2), jnp.where(longer_below, 1, 0))
        chunk = jnp.where(below == 1, me - distance, me + distance)
        return distance, below, chunk

    def rows_of(chunk):
        return pl.ds(pl.multiple_of(chunk * rows, rows), rows)

    def load(t):
        where = rows_of(at_step(t)[2])
        return (
            pltpu.make_async_copy(
                tau_hbm.at[0, :, :, where], tau.at[:, :, where], load_sem.at[0, t]
            ),
            pltpu.make_async_copy(
                beta_hbm.at[0, :, where, :], beta.at[:, where, :], load_sem.at[1, t]
            ),
        )

    own_tile = pltpu.make_async_copy(tile_hbm.at[0, 0], tile, tile_sem)
    own_tile.start()

    barrier = pltpu.get_barrier_semaphore()
    peers = n_tp * n_blk

    cores = 2 if n_tp % 2 == 0 else 1
    core = lax.rem(tp, cores)
    sibling = tp + 1 - 2 * core

    def same_core(other_tp, other_blk):
        other = jnp.logical_or(other_tp != tp, other_blk != me)
        return jnp.logical_and(other, lax.rem(other_tp, cores) == core)

    def greet(k, _):
        other_tp, other_blk = lax.div(k, n_blk), lax.rem(k, n_blk)

        @pl.when(same_core(other_tp, other_blk))
        def _():
            pl.semaphore_signal(
                barrier, inc=1, device_id=(sec, other_tp, other_blk), device_id_type=MESH
            )

        return 0

    lax.fori_loop(0, peers, greet, 0)
    sec_next = lax.rem(sec + 1, n_sec)
    sec_back = lax.rem(sec + n_sec - 1, n_sec)
    greeted = peers // cores - 1
    if cores > 1:
        pl.semaphore_signal(barrier, inc=1, device_id=(sec, sibling, me), device_id_type=MESH)
        greeted += 1
    if n_sec > 1:
        pl.semaphore_signal(barrier, inc=1, device_id=(sec_next, tp, me), device_id_type=MESH)
        greeted += 1
    if n_sec > 2:
        pl.semaphore_signal(barrier, inc=1, device_id=(sec_back, tp, me), device_id_type=MESH)
        greeted += 1

    for t in range(n_blk):
        for copy in load(t):
            copy.start()

    own_tile.wait()
    lane = lax.broadcasted_iota(jnp.int32, (rows, width), 1)
    real = tile[0].astype(jnp.float32)
    imag = tile[1].astype(jnp.float32)
    gathered[0, rows_of(me), :] = jnp.where(
        lane < half, real, pltpu.roll(imag, half, 1)
    ).astype(jnp.bfloat16)
    gathered[1, rows_of(me), :] = jnp.where(
        lane < half, pltpu.roll(real, half, 1), imag
    ).astype(jnp.bfloat16)
    image[...] = jnp.zeros_like(image)
    dense = n_tp * n_tp <= slots
    if dense:
        counts = [[jnp.float32(0)] * n_tp for _ in range(n_tp)]
        for g in range(slots):
            left, right = diagrams[0, 0, g], diagrams[0, 1, g]
            live = g < loads[0]
            for a in range(n_tp):
                in_a = jnp.where(jnp.logical_and(live, left == a), 1.0, 0.0)
                for b in range(n_tp):
                    counts[a][b] = counts[a][b] + jnp.where(right == b, in_a, 0.0)
    conj_w[...] = jnp.zeros_like(conj_w)
    pl.semaphore_wait(barrier, greeted)

    def pass_on(upward, distance, part, r):
        chunk = jnp.where(upward == 1, me - distance, me + distance)
        target = jnp.where(upward == 1, me + 1, me - 1)
        where = pl.ds(pl.multiple_of(chunk * rows + r * piece, piece), piece)
        block = gathered.at[part, where, :]
        return pltpu.make_async_remote_copy(
            src_ref=block,
            dst_ref=block,
            send_sem=send_sem.at[upward, distance, part, r],
            recv_sem=recv_sem.at[upward, distance, part, r],
            device_id=(sec, tp, target),
            device_id_type=MESH,
        )

    def arrival(below, distance, part, r):
        chunk = jnp.where(below == 1, me - distance, me + distance)
        where = pl.ds(pl.multiple_of(chunk * rows + r * piece, piece), piece)
        block = gathered.at[part, where, :]
        return pltpu.make_async_remote_copy(
            src_ref=block,
            dst_ref=block,
            send_sem=send_sem.at[below, distance, part, r],
            recv_sem=recv_sem.at[below, distance - 1, part, r],
            device_id=(sec, tp, me),
            device_id_type=MESH,
        )

    def send_own(upward, part):
        for r in range(PIECES):
            pass_on(upward, 0, part, r).start()

    for part in range(PARTS):
        @pl.when(me < n_blk - 1)
        def _():
            send_own(1, part)

        @pl.when(me > 0)
        def _():
            send_own(0, part)

    def w_copy(part):
        return pltpu.make_async_remote_copy(
            src_ref=w_send.at[part],
            dst_ref=w_recv.at[part],
            send_sem=w_send_sem.at[part],
            recv_sem=w_recv_sem.at[part],
            device_id=(sec_next, tp, me),
            device_id_type=MESH,
        )

    piece_lane = lax.broadcasted_iota(jnp.int32, (piece, width), 1)
    for part in range(PARTS):
        def receive(u):
            t, r = lax.div(u, PIECES), lax.rem(u, PIECES)
            distance, below, chunk = at_step(t)

            @pl.when(jnp.logical_and(t > 0, u < n_blk * PIECES))
            def _():
                arrival(below, distance, part, r).wait_recv()
                more = jnp.where(below == 1, me < n_blk - 1, me > 0)

                @pl.when(more)
                def _():
                    pass_on(below, distance, part, r).start()

        def step(u, _):
            t, r = lax.div(u, PIECES), lax.rem(u, PIECES)
            chunk = at_step(t)[2]

            @pl.when(both > 0)
            def _():
                receive(u + 1)

            if part == 0:
                @pl.when(r == 0)
                def _():
                    for copy in load(t):
                        copy.wait()

            where = pl.ds(pl.multiple_of(chunk * rows + r * piece, piece), piece)
            straight = gathered[part, where, :]
            wide = straight.astype(jnp.float32)
            turned = pltpu.roll(wide, half, 1)
            turned = jnp.where(piece_lane < half, -turned, turned)
            crossed = turned.astype(jnp.bfloat16)
            image[part] += jnp.dot(
                tau[0, :, where], straight, preferred_element_type=jnp.float32
            ) + jnp.dot(tau[1, :, where], crossed, preferred_element_type=jnp.float32)
            conj_w[part] += jnp.dot(
                wide.T.astype(jnp.bfloat16),
                beta[0, where, :],
                preferred_element_type=jnp.float32,
            ) + jnp.dot(
                (-turned).T.astype(jnp.bfloat16),
                beta[1, where, :],
                preferred_element_type=jnp.float32,
            )

            @pl.when(both == 0)
            def _():
                receive(u + 1)

            return 0

        lax.fori_loop(0, n_blk * PIECES, step, 0)
        if n_sec > 1:
            w_send[part] = conj_w[part].astype(jnp.bfloat16)
            w_copy(part).start()
        else:
            w_recv[part] = conj_w[part].astype(jnp.bfloat16)

    first, second = image[0], image[1]
    image_full[:, :width] = jnp.where(
        lane < half, first, pltpu.roll(second, half, 1)
    ).astype(jnp.bfloat16)
    image_full[:, width:] = jnp.where(
        lane < half, pltpu.roll(first, half, 1), second
    ).astype(jnp.bfloat16)

    share = half // n_blk

    def share_copy(part, distance):
        target = lax.rem(me + distance, n_blk)
        where = pl.ds(pl.multiple_of(target * share, share), share)
        return pltpu.make_async_remote_copy(
            src_ref=partial.at[part, :, where, :],
            dst_ref=shares.at[part, distance - 1],
            send_sem=share_send_sem.at[part, distance - 1],
            recv_sem=share_recv_sem.at[part, distance - 1],
            device_id=(sec, tp, target),
            device_id_type=MESH,
        )

    def block_copy(part, from_tp, from_blk, to_tp, to_blk, sem):
        slot = blocks.at[from_tp, part * n_blk + from_blk]
        return pltpu.make_async_remote_copy(
            src_ref=slot,
            dst_ref=slot,
            send_sem=sem,
            recv_sem=block_recv_sem.at[part, from_tp, from_blk],
            device_id=(sec, to_tp, to_blk),
            device_id_type=MESH,
        )

    def own_block(part, k):
        other_tp, other_blk = lax.div(k, n_blk), lax.rem(k, n_blk)
        sem = block_send_sem.at[part, other_tp, other_blk]
        copy = block_copy(part, tp, me, other_tp, other_blk, sem)
        return copy, same_core(other_tp, other_blk)

    def sibling_block(part, k):
        from_tp, from_blk = lax.div(k, n_blk), lax.rem(k, n_blk)
        sem = pair_send_sem.at[part, from_tp, from_blk]
        copy = block_copy(part, from_tp, from_blk, sibling, me, sem)
        return copy, lax.rem(from_tp, cores) == core

    def start_sum(part):
        if n_sec > 1:
            w_copy(part).wait_recv()
        product = jnp.dot(w_recv[part], image_full[...], preferred_element_type=jnp.float32)
        partial[part, 0] = (product[:half, :width] + product[half:, width:]).astype(jnp.bfloat16)
        partial[part, 1] = (product[:half, width:] - product[half:, :width]).astype(jnp.bfloat16)
        for distance in range(1, n_blk):
            share_copy(part, distance).start()

    def end_sum(part):
        where = pl.ds(pl.multiple_of(me * share, share), share)
        total = partial[part, :, where, :].astype(jnp.float32)
        for distance in range(1, n_blk):
            share_copy(part, distance).wait_recv()
            total = total + shares[part, distance - 1].astype(jnp.float32)
        blocks[tp, part * n_blk + me] = (total * order ** (-0.5)).astype(jnp.bfloat16)

        def start_block(k, _):
            copy, wanted = own_block(part, k)

            @pl.when(wanted)
            def _():
                copy.start()

            return 0

        lax.fori_loop(0, peers, start_block, 0)
        if cores > 1:
            block_copy(part, tp, me, sibling, me, pair_send_sem.at[part, tp, me]).start()

    def end_gather(part):
        def wait_block(k, _):
            other_tp, other_blk = lax.div(k, n_blk), lax.rem(k, n_blk)

            @pl.when(same_core(other_tp, other_blk))
            def _():
                sem = block_send_sem.at[part, other_tp, other_blk]
                block_copy(part, other_tp, other_blk, tp, me, sem).wait_recv()
                if cores > 1:
                    sibling_block(part, k)[0].start()

            return 0

        lax.fori_loop(0, peers, wait_block, 0)

    def end_pair(part):
        def wait_pair(k, _):
            copy, passed = sibling_block(part, k)

            @pl.when(jnp.logical_not(passed))
            def _():
                copy.wait_recv()

            return 0

        if cores > 1:
            lax.fori_loop(0, peers, wait_pair, 0)

    start_sum(0)
    for part in range(PARTS):
        end_sum(part)
        if part + 1 < PARTS:
            start_sum(part + 1)

    def drain(u, _):
        distance = lax.div(u, PIECES)
        r = lax.rem(u, PIECES)
        for part in range(PARTS):
            @pl.when(jnp.logical_and(distance <= me, me < n_blk - 1))
            def _():
                pass_on(1, distance, part, r).wait_send()

            @pl.when(jnp.logical_and(me + distance < n_blk, me > 0))
            def _():
                pass_on(0, distance, part, r).wait_send()

        return 0

    lax.fori_loop(0, n_blk * PIECES, drain, 0)
    if n_sec > 1:
        for part in range(PARTS):
            w_copy(part).wait_send()
    for part in range(PARTS):
        for distance in range(1, n_blk):
            share_copy(part, distance).wait_send()
    for part in range(PARTS):
        end_gather(part)
    for part in range(PARTS):
        end_pair(part)

    def right_of(index):
        right = blocks[index]
        return jnp.concatenate(
            [right[:, 0].reshape(width, width), right[:, 1].reshape(width, width)], axis=1
        )

    def left_of(index):
        left = blocks[index, pl.ds(pl.multiple_of(me * PARTS, PARTS), PARTS)].astype(jnp.float32)
        return jnp.concatenate(
            [left[:, 0].reshape(quarter, width), left[:, 1].reshape(quarter, width)], axis=0
        )

    if dense:
        lefts = [left_of(a) for a in range(n_tp)]
        sums = jnp.zeros((4 * quarter, 2 * width), jnp.float32)
        for b in range(n_tp):
            left = lefts[0] * counts[0][b]
            for a in range(1, n_tp):
                left = left + lefts[a] * counts[a][b]
            high = left.astype(jnp.bfloat16)
            low = (left - high.astype(jnp.float32)).astype(jnp.bfloat16)
            sums = sums + jnp.dot(
                jnp.concatenate([high, low], axis=0),
                right_of(b),
                preferred_element_type=jnp.float32,
            )
        sums = sums[: 2 * quarter] + sums[2 * quarter :]
    else:
        sums = jnp.zeros((2 * quarter, 2 * width), jnp.float32)
        for g in range(slots):
            active = jnp.where(g < loads[0], 1.0, 0.0)
            left = (left_of(diagrams[0, 0, g]) * active).astype(jnp.bfloat16)
            sums = sums + jnp.dot(
                left, right_of(diagrams[0, 1, g]), preferred_element_type=jnp.float32
            )
    scale = (width * slots) ** (-0.5)
    out[0, 0, 0] = (sums[:quarter, :width] - sums[quarter:, width:]) * scale
    out[0, 0, 1] = (sums[:quarter, width:] + sums[quarter:, :width]) * scale


    def drain_block(k, _):
        for part in range(PARTS):
            copy, sent = own_block(part, k)

            @pl.when(sent)
            def _():
                copy.wait_send()

            if cores > 1:
                pair_copy, passed = sibling_block(part, k)

                @pl.when(passed)
                def _():
                    pair_copy.wait_send()

        return 0

    lax.fori_loop(0, peers, drain_block, 0)


def on_device(n_sec, n_tp, n_blk, perambulator, backward, elementals, diagrams, owner_loads):
    rows, order = perambulator.shape[2:]
    width = elementals.shape[4]
    half = width // PARTS
    quarter = width // n_blk
    hbm = pl.BlockSpec(memory_space=pltpu.HBM)
    smem = pl.BlockSpec(memory_space=pltpu.SMEM)
    dma = pltpu.SemaphoreType.DMA
    return pl.pallas_call(
        functools.partial(kernel, n_sec, n_tp, n_blk),
        out_shape=jax.ShapeDtypeStruct((1, 1, 2, quarter, width), jnp.float32),
        in_specs=[hbm, hbm, hbm, smem, smem],
        out_specs=pl.BlockSpec(memory_space=pltpu.VMEM),
        scratch_shapes=[
            pltpu.VMEM((2, rows, order), jnp.bfloat16),
            pltpu.VMEM((2, order, rows), jnp.bfloat16),
            pltpu.VMEM((2, rows, width), jnp.bfloat16),
            pltpu.VMEM((PARTS, order, 2 * half), jnp.bfloat16),
            pltpu.VMEM((PARTS, rows, 2 * half), jnp.float32),
            pltpu.VMEM((PARTS, 2 * half, rows), jnp.float32),
            pltpu.VMEM((PARTS, 2 * half, rows), jnp.bfloat16),
            pltpu.VMEM((PARTS, 2 * half, rows), jnp.bfloat16),
            pltpu.VMEM((rows, 2 * width), jnp.bfloat16),
            pltpu.VMEM((PARTS, 2, half, width), jnp.bfloat16),
            pltpu.VMEM((PARTS, n_blk, 2, half // n_blk, width), jnp.bfloat16),
            pltpu.VMEM((n_tp, PARTS * n_blk, 2, half // n_blk, width), jnp.bfloat16),
            dma((2, n_blk)),
            dma,
            dma((2, n_blk, PARTS, PIECES)),
            dma((2, n_blk, PARTS, PIECES)),
            dma((PARTS,)),
            dma((PARTS,)),
            dma((PARTS, n_blk)),
            dma((PARTS, n_blk)),
            dma((PARTS, n_tp, n_blk)),
            dma((PARTS, n_tp, n_blk)),
            dma((PARTS, n_tp, n_blk)),
        ],
        compiler_params=pltpu.CompilerParams(
            collective_id=0, has_side_effects=True, vmem_limit_bytes=60 * 1024 * 1024
        ),
    )(perambulator, backward, elementals, jnp.swapaxes(diagrams, 1, 2), owner_loads)


def solution(mesh):
    placed = (
        P("tp", None, "blk", None),
        P("tp", None, None, "blk"),
        P("sec", "tp", None, "blk", None),
        P("tp", None, None),
        P("tp"),
    )
    sizes = (mesh.shape["sec"], mesh.shape["tp"], mesh.shape["blk"])
    return jax.shard_map(
        functools.partial(on_device, *sizes),
        mesh=mesh,
        in_specs=placed,
        out_specs=P("sec", "tp", None, "blk", None),
        check_vma=False,
    )
```

```python
import functools

import jax
import jax.numpy as jnp
from jax import lax
from jax.experimental import pallas as pl
from jax.experimental.pallas import tpu as pltpu
from jax.sharding import PartitionSpec as P

PARTS = 2
PIECES = 2
MESH = pl.DeviceIdType.MESH


def kernel(
    n_sec, n_tp, n_blk,
    tau_hbm, beta_hbm, tile_hbm, diagrams, loads, out,
    tau, beta, tile, gathered, image, conj_w, w_send, w_recv, image_full,
    partial, shares, blocks,
    load_sem, tile_sem, send_sem, recv_sem, w_send_sem, w_recv_sem,
    share_send_sem, share_recv_sem, block_send_sem, block_recv_sem,
):
    sec, tp, me = lax.axis_index("sec"), lax.axis_index("tp"), lax.axis_index("blk")
    rows, order = tau_hbm.shape[2], tau_hbm.shape[3]
    width = tile_hbm.shape[4]
    half = width // PARTS
    piece = rows // PIECES
    quarter = width // n_blk
    slots = diagrams.shape[2]

    both = jnp.minimum(me, n_blk - 1 - me)
    longer_below = me > n_blk - 1 - me

    def at_step(t):
        in_both = t <= 2 * both
        distance = jnp.where(in_both, lax.div(t + 1, 2), t - both)
        below = jnp.where(in_both, lax.rem(t, 2), jnp.where(longer_below, 1, 0))
        chunk = jnp.where(below == 1, me - distance, me + distance)
        return distance, below, chunk

    def rows_of(chunk):
        return pl.ds(pl.multiple_of(chunk * rows, rows), rows)

    def load(t):
        where = rows_of(at_step(t)[2])
        return (
            pltpu.make_async_copy(
                tau_hbm.at[0, :, :, where], tau.at[:, :, where], load_sem.at[0, t]
            ),
            pltpu.make_async_copy(
                beta_hbm.at[0, :, where, :], beta.at[:, where, :], load_sem.at[1, t]
            ),
        )

    own_tile = pltpu.make_async_copy(tile_hbm.at[0, 0], tile, tile_sem)
    own_tile.start()

    barrier = pltpu.get_barrier_semaphore()
    peers = n_tp * n_blk

    def each_peer(visit):
        def at(k):
            other_tp = lax.rem(tp + lax.div(k, n_blk), n_tp)
            other_blk = lax.rem(me + lax.rem(k, n_blk), n_blk)
            visit(other_tp, other_blk)

        if peers <= 16:
            for k in range(peers - 1, 0, -1):
                at(jnp.int32(k))
        else:
            lax.fori_loop(1, peers, lambda k, _: (at(k), 0)[1], 0)

    def greet(other_tp, other_blk):
        pl.semaphore_signal(
            barrier, inc=1, device_id=(sec, other_tp, other_blk), device_id_type=MESH
        )

    each_peer(greet)
    sec_next = lax.rem(sec + 1, n_sec)
    sec_back = lax.rem(sec + n_sec - 1, n_sec)
    greeted = peers - 1
    if n_sec > 1:
        pl.semaphore_signal(barrier, inc=1, device_id=(sec_next, tp, me), device_id_type=MESH)
        greeted += 1
    if n_sec > 2:
        pl.semaphore_signal(barrier, inc=1, device_id=(sec_back, tp, me), device_id_type=MESH)
        greeted += 1

    for t in range(n_blk):
        for copy in load(t):
            copy.start()

    own_tile.wait()
    lane = lax.broadcasted_iota(jnp.int32, (rows, width), 1)
    real = tile[0].astype(jnp.float32)
    imag = tile[1].astype(jnp.float32)
    gathered[0, rows_of(me), :] = jnp.where(
        lane < half, real, pltpu.roll(imag, half, 1)
    ).astype(jnp.bfloat16)
    gathered[1, rows_of(me), :] = jnp.where(
        lane < half, pltpu.roll(real, half, 1), imag
    ).astype(jnp.bfloat16)
    image[...] = jnp.zeros_like(image)
    dense = n_tp * n_tp <= slots
    if dense:
        counts = [[jnp.float32(0)] * n_tp for _ in range(n_tp)]
        for g in range(slots):
            left, right = diagrams[0, 0, g], diagrams[0, 1, g]
            live = g < loads[0]
            for a in range(n_tp):
                in_a = jnp.where(jnp.logical_and(live, left == a), 1.0, 0.0)
                for b in range(n_tp):
                    counts[a][b] = counts[a][b] + jnp.where(right == b, in_a, 0.0)
    conj_w[...] = jnp.zeros_like(conj_w)
    pl.semaphore_wait(barrier, greeted)

    def pass_on(upward, distance, part, r):
        chunk = jnp.where(upward == 1, me - distance, me + distance)
        target = jnp.where(upward == 1, me + 1, me - 1)
        where = pl.ds(pl.multiple_of(chunk * rows + r * piece, piece), piece)
        block = gathered.at[part, where, :]
        return pltpu.make_async_remote_copy(
            src_ref=block,
            dst_ref=block,
            send_sem=send_sem.at[upward, distance, part, r],
            recv_sem=recv_sem.at[upward, distance, part, r],
            device_id=(sec, tp, target),
            device_id_type=MESH,
        )

    def arrival(below, distance, part, r):
        chunk = jnp.where(below == 1, me - distance, me + distance)
        where = pl.ds(pl.multiple_of(chunk * rows + r * piece, piece), piece)
        block = gathered.at[part, where, :]
        return pltpu.make_async_remote_copy(
            src_ref=block,
            dst_ref=block,
            send_sem=send_sem.at[below, distance, part, r],
            recv_sem=recv_sem.at[below, distance - 1, part, r],
            device_id=(sec, tp, me),
            device_id_type=MESH,
        )

    def send_own(upward, part):
        for r in range(PIECES):
            pass_on(upward, 0, part, r).start()

    for part in range(PARTS):
        @pl.when(me < n_blk - 1)
        def _():
            send_own(1, part)

        @pl.when(me > 0)
        def _():
            send_own(0, part)

    def w_copy(part):
        return pltpu.make_async_remote_copy(
            src_ref=w_send.at[part],
            dst_ref=w_recv.at[part],
            send_sem=w_send_sem.at[part],
            recv_sem=w_recv_sem.at[part],
            device_id=(sec_next, tp, me),
            device_id_type=MESH,
        )

    piece_lane = lax.broadcasted_iota(jnp.int32, (piece, width), 1)
    for part in range(PARTS):
        def receive(u):
            t, r = lax.div(u, PIECES), lax.rem(u, PIECES)
            distance, below, chunk = at_step(t)

            @pl.when(jnp.logical_and(t > 0, u < n_blk * PIECES))
            def _():
                arrival(below, distance, part, r).wait_recv()
                more = jnp.where(below == 1, me < n_blk - 1, me > 0)

                @pl.when(more)
                def _():
                    pass_on(below, distance, part, r).start()

        def step(u, _):
            t, r = lax.div(u, PIECES), lax.rem(u, PIECES)
            chunk = at_step(t)[2]

            @pl.when(both > 0)
            def _():
                receive(u + 1)

            if part == 0:
                @pl.when(r == 0)
                def _():
                    for copy in load(t):
                        copy.wait()

            where = pl.ds(pl.multiple_of(chunk * rows + r * piece, piece), piece)
            straight = gathered[part, where, :]
            wide = straight.astype(jnp.float32)
            turned = pltpu.roll(wide, half, 1)
            turned = jnp.where(piece_lane < half, -turned, turned)
            crossed = turned.astype(jnp.bfloat16)
            image[part] += jnp.dot(
                tau[0, :, where], straight, preferred_element_type=jnp.float32
            ) + jnp.dot(tau[1, :, where], crossed, preferred_element_type=jnp.float32)
            conj_w[part] += jnp.dot(
                wide.T.astype(jnp.bfloat16),
                beta[0, where, :],
                preferred_element_type=jnp.float32,
            ) + jnp.dot(
                (-turned).T.astype(jnp.bfloat16),
                beta[1, where, :],
                preferred_element_type=jnp.float32,
            )

            @pl.when(both == 0)
            def _():
                receive(u + 1)

            return 0

        lax.fori_loop(0, n_blk * PIECES, step, 0)
        if n_sec > 1:
            w_send[part] = conj_w[part].astype(jnp.bfloat16)
            w_copy(part).start()
        else:
            w_recv[part] = conj_w[part].astype(jnp.bfloat16)

    first, second = image[0], image[1]
    image_full[:, :width] = jnp.where(
        lane < half, first, pltpu.roll(second, half, 1)
    ).astype(jnp.bfloat16)
    image_full[:, width:] = jnp.where(
        lane < half, pltpu.roll(first, half, 1), second
    ).astype(jnp.bfloat16)

    share = half // n_blk

    def share_copy(part, distance):
        target = lax.rem(me + distance, n_blk)
        where = pl.ds(pl.multiple_of(target * share, share), share)
        return pltpu.make_async_remote_copy(
            src_ref=partial.at[part, :, where, :],
            dst_ref=shares.at[part, distance - 1],
            send_sem=share_send_sem.at[part],
            recv_sem=share_recv_sem.at[part],
            device_id=(sec, tp, target),
            device_id_type=MESH,
        )

    def all_shares(part):
        every = shares.at[part]
        return pltpu.make_async_remote_copy(
            src_ref=every,
            dst_ref=every,
            send_sem=share_send_sem.at[part],
            recv_sem=share_recv_sem.at[part],
            device_id=(sec, tp, me),
            device_id_type=MESH,
        )

    def block_copy(part, slot, other_tp, other_blk):
        return pltpu.make_async_remote_copy(
            src_ref=slot,
            dst_ref=slot,
            send_sem=block_send_sem.at[part],
            recv_sem=block_recv_sem.at[part],
            device_id=(sec, other_tp, other_blk),
            device_id_type=MESH,
        )

    def all_blocks(part):
        return block_copy(part, blocks.at[part, pl.ds(0, peers - 1)], tp, me)

    def start_sum(part):
        if n_sec > 1:
            w_copy(part).wait_recv()
        product = jnp.dot(w_recv[part], image_full[...], preferred_element_type=jnp.float32)
        partial[part, 0] = (product[:half, :width] + product[half:, width:]).astype(jnp.bfloat16)
        partial[part, 1] = (product[:half, width:] - product[half:, :width]).astype(jnp.bfloat16)
        for distance in range(1, n_blk):
            share_copy(part, distance).start()

    def end_sum(part):
        where = pl.ds(pl.multiple_of(me * share, share), share)
        total = partial[part, :, where, :].astype(jnp.float32)
        all_shares(part).wait_recv()
        for distance in range(1, n_blk):
            total = total + shares[part, distance - 1].astype(jnp.float32)
        own = tp * n_blk + me
        blocks[part, own] = (total * order ** (-0.5)).astype(jnp.bfloat16)
        each_peer(lambda *other: block_copy(part, blocks.at[part, own], *other).start())

    start_sum(0)
    for part in range(PARTS):
        end_sum(part)
        if part + 1 < PARTS:
            start_sum(part + 1)

    def drain(u, _):
        distance = lax.div(u, PIECES)
        r = lax.rem(u, PIECES)
        for part in range(PARTS):
            @pl.when(jnp.logical_and(distance <= me, me < n_blk - 1))
            def _():
                pass_on(1, distance, part, r).wait_send()

            @pl.when(jnp.logical_and(me + distance < n_blk, me > 0))
            def _():
                pass_on(0, distance, part, r).wait_send()

        return 0

    lax.fori_loop(0, n_blk * PIECES, drain, 0)
    if n_sec > 1:
        for part in range(PARTS):
            w_copy(part).wait_send()
    for part in range(PARTS):
        all_shares(part).wait_send()
    for part in range(PARTS):
        all_blocks(part).wait_recv()

    def right_of(index):
        first = index * n_blk
        right = blocks[:, pl.ds(first, n_blk)].reshape(PARTS * n_blk, 2, share, width)
        return jnp.concatenate(
            [right[:, 0].reshape(width, width), right[:, 1].reshape(width, width)], axis=1
        )

    def left_of(index):
        first = me * PARTS
        at = index * n_blk + lax.rem(first, n_blk)
        left = blocks[lax.div(first, n_blk), pl.ds(at, PARTS)].astype(jnp.float32)
        return jnp.concatenate(
            [left[:, 0].reshape(quarter, width), left[:, 1].reshape(quarter, width)], axis=0
        )

    if dense:
        lefts = [left_of(a) for a in range(n_tp)]
        sums = jnp.zeros((4 * quarter, 2 * width), jnp.float32)
        for b in range(n_tp):
            left = lefts[0] * counts[0][b]
            for a in range(1, n_tp):
                left = left + lefts[a] * counts[a][b]
            high = left.astype(jnp.bfloat16)
            low = (left - high.astype(jnp.float32)).astype(jnp.bfloat16)
            sums = sums + jnp.dot(
                jnp.concatenate([high, low], axis=0),
                right_of(b),
                preferred_element_type=jnp.float32,
            )
        sums = sums[: 2 * quarter] + sums[2 * quarter :]
    else:
        sums = jnp.zeros((2 * quarter, 2 * width), jnp.float32)
        for g in range(slots):
            active = jnp.where(g < loads[0], 1.0, 0.0)
            left = (left_of(diagrams[0, 0, g]) * active).astype(jnp.bfloat16)
            sums = sums + jnp.dot(
                left, right_of(diagrams[0, 1, g]), preferred_element_type=jnp.float32
            )
    scale = (width * slots) ** (-0.5)
    out[0, 0, 0] = (sums[:quarter, :width] - sums[quarter:, width:]) * scale
    out[0, 0, 1] = (sums[:quarter, width:] + sums[quarter:, :width]) * scale


    for part in range(PARTS):
        all_blocks(part).wait_send()


def on_device(n_sec, n_tp, n_blk, perambulator, backward, elementals, diagrams, owner_loads):
    rows, order = perambulator.shape[2:]
    width = elementals.shape[4]
    half = width // PARTS
    quarter = width // n_blk
    hbm = pl.BlockSpec(memory_space=pltpu.HBM)
    smem = pl.BlockSpec(memory_space=pltpu.SMEM)
    dma = pltpu.SemaphoreType.DMA
    return pl.pallas_call(
        functools.partial(kernel, n_sec, n_tp, n_blk),
        out_shape=jax.ShapeDtypeStruct((1, 1, 2, quarter, width), jnp.float32),
        in_specs=[hbm, hbm, hbm, smem, smem],
        out_specs=pl.BlockSpec(memory_space=pltpu.VMEM),
        scratch_shapes=[
            pltpu.VMEM((2, rows, order), jnp.bfloat16),
            pltpu.VMEM((2, order, rows), jnp.bfloat16),
            pltpu.VMEM((2, rows, width), jnp.bfloat16),
            pltpu.VMEM((PARTS, order, 2 * half), jnp.bfloat16),
            pltpu.VMEM((PARTS, rows, 2 * half), jnp.float32),
            pltpu.VMEM((PARTS, 2 * half, rows), jnp.float32),
            pltpu.VMEM((PARTS, 2 * half, rows), jnp.bfloat16),
            pltpu.VMEM((PARTS, 2 * half, rows), jnp.bfloat16),
            pltpu.VMEM((rows, 2 * width), jnp.bfloat16),
            pltpu.VMEM((PARTS, 2, half, width), jnp.bfloat16),
            pltpu.VMEM((PARTS, n_blk - 1, 2, half // n_blk, width), jnp.bfloat16),
            pltpu.VMEM((PARTS, n_tp * n_blk, 2, half // n_blk, width), jnp.bfloat16),
            dma((2, n_blk)),
            dma,
            dma((2, n_blk, PARTS, PIECES)),
            dma((2, n_blk, PARTS, PIECES)),
            dma((PARTS,)),
            dma((PARTS,)),
            dma((PARTS,)),
            dma((PARTS,)),
            dma((PARTS,)),
            dma((PARTS,)),
        ],
        compiler_params=pltpu.CompilerParams(
            collective_id=0, has_side_effects=True, vmem_limit_bytes=60 * 1024 * 1024
        ),
    )(perambulator, backward, elementals, jnp.swapaxes(diagrams, 1, 2), owner_loads)


def solution(mesh):
    placed = (
        P("tp", None, "blk", None),
        P("tp", None, None, "blk"),
        P("sec", "tp", None, "blk", None),
        P("tp", None, None),
        P("tp"),
    )
    sizes = (mesh.shape["sec"], mesh.shape["tp"], mesh.shape["blk"])
    return jax.shard_map(
        functools.partial(on_device, *sizes),
        mesh=mesh,
        in_specs=placed,
        out_specs=P("sec", "tp", None, "blk", None),
        check_vma=False,
    )
```

```python
import functools

import jax
import jax.numpy as jnp
from jax import lax
from jax.experimental import pallas as pl
from jax.experimental.pallas import tpu as pltpu
from jax.sharding import PartitionSpec as P

PARTS = 2
PIECES = 2
MESH = pl.DeviceIdType.MESH


def kernel(
    n_sec, n_tp, n_blk,
    tau_hbm, beta_hbm, tile_hbm, diagrams, loads, out,
    tau, beta, tile, gathered, image, conj_w, w_send, w_recv, image_full,
    partial, shares, blocks,
    load_sem, tile_sem, send_sem, recv_sem, w_send_sem, w_recv_sem,
    share_send_sem, share_recv_sem, block_send_sem, block_recv_sem,
):
    sec, tp, me = lax.axis_index("sec"), lax.axis_index("tp"), lax.axis_index("blk")
    rows, order = tau_hbm.shape[2], tau_hbm.shape[3]
    width = tile_hbm.shape[4]
    half = width // PARTS
    piece = rows // PIECES
    quarter = width // n_blk
    slots = diagrams.shape[2]

    both = jnp.minimum(me, n_blk - 1 - me)
    longer_below = me > n_blk - 1 - me

    def at_step(t):
        in_both = t <= 2 * both
        distance = jnp.where(in_both, lax.div(t + 1, 2), t - both)
        below = jnp.where(in_both, lax.rem(t, 2), jnp.where(longer_below, 1, 0))
        chunk = jnp.where(below == 1, me - distance, me + distance)
        return distance, below, chunk

    def rows_of(chunk):
        return pl.ds(pl.multiple_of(chunk * rows, rows), rows)

    def load(t):
        where = rows_of(at_step(t)[2])
        return (
            pltpu.make_async_copy(
                tau_hbm.at[0, :, :, where], tau.at[:, :, where], load_sem.at[0, t]
            ),
            pltpu.make_async_copy(
                beta_hbm.at[0, :, where, :], beta.at[:, where, :], load_sem.at[1, t]
            ),
        )

    own_tile = pltpu.make_async_copy(tile_hbm.at[0, 0], tile, tile_sem)
    own_tile.start()

    barrier = pltpu.get_barrier_semaphore()
    peers = n_tp * n_blk

    def each_peer(visit):
        def at(k):
            other_tp = lax.rem(tp + lax.div(k, n_blk), n_tp)
            other_blk = lax.rem(me + lax.rem(k, n_blk), n_blk)
            visit(other_tp, other_blk)

        if peers <= 16:
            for k in range(peers - 1, 0, -1):
                at(jnp.int32(k))
        else:
            lax.fori_loop(1, peers, lambda k, _: (at(k), 0)[1], 0)

    def greet(other_tp, other_blk):
        pl.semaphore_signal(
            barrier, inc=1, device_id=(sec, other_tp, other_blk), device_id_type=MESH
        )

    each_peer(greet)
    sec_next = lax.rem(sec + 1, n_sec)
    sec_back = lax.rem(sec + n_sec - 1, n_sec)
    greeted = peers - 1
    if n_sec > 1:
        pl.semaphore_signal(barrier, inc=1, device_id=(sec_next, tp, me), device_id_type=MESH)
        greeted += 1
    if n_sec > 2:
        pl.semaphore_signal(barrier, inc=1, device_id=(sec_back, tp, me), device_id_type=MESH)
        greeted += 1

    for t in range(n_blk):
        for copy in load(t):
            copy.start()

    own_tile.wait()
    lane = lax.broadcasted_iota(jnp.int32, (rows, width), 1)
    real = tile[0].astype(jnp.float32)
    imag = tile[1].astype(jnp.float32)
    gathered[0, rows_of(me), :] = jnp.where(
        lane < half, real, pltpu.roll(imag, half, 1)
    ).astype(jnp.bfloat16)
    gathered[1, rows_of(me), :] = jnp.where(
        lane < half, pltpu.roll(real, half, 1), imag
    ).astype(jnp.bfloat16)
    image[...] = jnp.zeros_like(image)
    dense = n_tp * n_tp <= slots
    if dense:
        counts = [[jnp.float32(0)] * n_tp for _ in range(n_tp)]
        for g in range(slots):
            left, right = diagrams[0, 0, g], diagrams[0, 1, g]
            live = g < loads[0]
            for a in range(n_tp):
                in_a = jnp.where(jnp.logical_and(live, left == a), 1.0, 0.0)
                for b in range(n_tp):
                    counts[a][b] = counts[a][b] + jnp.where(right == b, in_a, 0.0)
    conj_w[...] = jnp.zeros_like(conj_w)
    pl.semaphore_wait(barrier, greeted)

    def pass_on(upward, distance, part, r):
        chunk = jnp.where(upward == 1, me - distance, me + distance)
        target = jnp.where(upward == 1, me + 1, me - 1)
        where = pl.ds(pl.multiple_of(chunk * rows + r * piece, piece), piece)
        block = gathered.at[part, where, :]
        return pltpu.make_async_remote_copy(
            src_ref=block,
            dst_ref=block,
            send_sem=send_sem.at[upward, distance, part, r],
            recv_sem=recv_sem.at[upward, distance, part, r],
            device_id=(sec, tp, target),
            device_id_type=MESH,
        )

    def arrival(below, distance, part, r):
        chunk = jnp.where(below == 1, me - distance, me + distance)
        where = pl.ds(pl.multiple_of(chunk * rows + r * piece, piece), piece)
        block = gathered.at[part, where, :]
        return pltpu.make_async_remote_copy(
            src_ref=block,
            dst_ref=block,
            send_sem=send_sem.at[below, distance, part, r],
            recv_sem=recv_sem.at[below, distance - 1, part, r],
            device_id=(sec, tp, me),
            device_id_type=MESH,
        )

    def send_own(upward, part):
        for r in range(PIECES):
            pass_on(upward, 0, part, r).start()

    for part in range(PARTS):
        @pl.when(me < n_blk - 1)
        def _():
            send_own(1, part)

        @pl.when(me > 0)
        def _():
            send_own(0, part)

    def w_copy(part):
        return pltpu.make_async_remote_copy(
            src_ref=w_send.at[part],
            dst_ref=w_recv.at[part],
            send_sem=w_send_sem.at[part],
            recv_sem=w_recv_sem.at[part],
            device_id=(sec_next, tp, me),
            device_id_type=MESH,
        )

    for part in range(PARTS):
        def receive(t):
            distance, below, _ = at_step(t)

            @pl.when(jnp.logical_and(t > 0, t < n_blk))
            def _():
                more = jnp.where(below == 1, me < n_blk - 1, me > 0)
                for r in range(PIECES):
                    arrival(below, distance, part, r).wait_recv()

                    @pl.when(more)
                    def _():
                        pass_on(below, distance, part, r).start()

        def step(t, _):
            @pl.when(both > 0)
            def _():
                receive(t + 1)

            if part == 0:
                for copy in load(t):
                    copy.wait()

            where = rows_of(at_step(t)[2])
            straight = gathered[part, where, :]
            turned = pltpu.roll(straight.astype(jnp.float32), half, 1)
            crossed = jnp.where(lane < half, -turned, turned).astype(jnp.bfloat16)
            image[part] += jnp.dot(
                jnp.concatenate([tau[0, :, where], tau[1, :, where]], axis=1),
                jnp.concatenate([straight, crossed], axis=0),
                preferred_element_type=jnp.float32,
            )
            upright = straight.T
            upright = jnp.concatenate(
                [upright, jnp.concatenate([upright[half:], -upright[:half]], axis=0)], axis=1
            )
            conj_w[part] += jnp.dot(
                upright,
                jnp.concatenate([beta[0, where, :], beta[1, where, :]], axis=0),
                preferred_element_type=jnp.float32,
            )

            @pl.when(both == 0)
            def _():
                receive(t + 1)

            return 0

        lax.fori_loop(0, n_blk, step, 0)
        if n_sec > 1:
            w_send[part] = conj_w[part].astype(jnp.bfloat16)
            w_copy(part).start()
        else:
            w_recv[part] = conj_w[part].astype(jnp.bfloat16)

    first, second = image[0], image[1]
    image_full[:, :width] = jnp.where(
        lane < half, first, pltpu.roll(second, half, 1)
    ).astype(jnp.bfloat16)
    image_full[:, width:] = jnp.where(
        lane < half, pltpu.roll(first, half, 1), second
    ).astype(jnp.bfloat16)

    share = half // n_blk

    def share_copy(part, distance):
        target = lax.rem(me + distance, n_blk)
        where = pl.ds(pl.multiple_of(target * share, share), share)
        return pltpu.make_async_remote_copy(
            src_ref=partial.at[part, :, where, :],
            dst_ref=shares.at[part, distance - 1],
            send_sem=share_send_sem.at[part],
            recv_sem=share_recv_sem.at[part],
            device_id=(sec, tp, target),
            device_id_type=MESH,
        )

    def all_shares(part):
        every = shares.at[part]
        return pltpu.make_async_remote_copy(
            src_ref=every,
            dst_ref=every,
            send_sem=share_send_sem.at[part],
            recv_sem=share_recv_sem.at[part],
            device_id=(sec, tp, me),
            device_id_type=MESH,
        )

    def block_copy(part, slot, other_tp, other_blk):
        return pltpu.make_async_remote_copy(
            src_ref=slot,
            dst_ref=slot,
            send_sem=block_send_sem.at[part],
            recv_sem=block_recv_sem.at[part],
            device_id=(sec, other_tp, other_blk),
            device_id_type=MESH,
        )

    def all_blocks(part):
        return block_copy(part, blocks.at[part, pl.ds(0, peers - 1)], tp, me)

    def start_sum(part):
        if n_sec > 1:
            w_copy(part).wait_recv()
        product = jnp.dot(w_recv[part], image_full[...], preferred_element_type=jnp.float32)
        partial[part, 0] = (product[:half, :width] + product[half:, width:]).astype(jnp.bfloat16)
        partial[part, 1] = (product[:half, width:] - product[half:, :width]).astype(jnp.bfloat16)
        for distance in range(1, n_blk):
            share_copy(part, distance).start()

    def end_sum(part):
        where = pl.ds(pl.multiple_of(me * share, share), share)
        total = partial[part, :, where, :].astype(jnp.float32)
        all_shares(part).wait_recv()
        for distance in range(1, n_blk):
            total = total + shares[part, distance - 1].astype(jnp.float32)
        own = tp * n_blk + me
        blocks[part, own] = (total * order ** (-0.5)).astype(jnp.bfloat16)
        each_peer(lambda *other: block_copy(part, blocks.at[part, own], *other).start())

    start_sum(0)
    for part in range(PARTS):
        end_sum(part)
        if part + 1 < PARTS:
            start_sum(part + 1)

    def drain(u, _):
        distance = lax.div(u, PIECES)
        r = lax.rem(u, PIECES)
        for part in range(PARTS):
            @pl.when(jnp.logical_and(distance <= me, me < n_blk - 1))
            def _():
                pass_on(1, distance, part, r).wait_send()

            @pl.when(jnp.logical_and(me + distance < n_blk, me > 0))
            def _():
                pass_on(0, distance, part, r).wait_send()

        return 0

    lax.fori_loop(0, n_blk * PIECES, drain, 0)
    if n_sec > 1:
        for part in range(PARTS):
            w_copy(part).wait_send()
    for part in range(PARTS):
        all_shares(part).wait_send()
    for part in range(PARTS):
        all_blocks(part).wait_recv()

    def right_of(index):
        first = index * n_blk
        right = blocks[:, pl.ds(first, n_blk)].reshape(PARTS * n_blk, 2, share, width)
        return jnp.concatenate(
            [right[:, 0].reshape(width, width), right[:, 1].reshape(width, width)], axis=1
        )

    def left_of(index):
        first = me * PARTS
        at = index * n_blk + lax.rem(first, n_blk)
        left = blocks[lax.div(first, n_blk), pl.ds(at, PARTS)].astype(jnp.float32)
        return jnp.concatenate(
            [left[:, 0].reshape(quarter, width), left[:, 1].reshape(quarter, width)], axis=0
        )

    if dense:
        lefts = [left_of(a) for a in range(n_tp)]
        sums = jnp.zeros((4 * quarter, 2 * width), jnp.float32)
        for b in range(n_tp):
            left = lefts[0] * counts[0][b]
            for a in range(1, n_tp):
                left = left + lefts[a] * counts[a][b]
            high = left.astype(jnp.bfloat16)
            low = (left - high.astype(jnp.float32)).astype(jnp.bfloat16)
            sums = sums + jnp.dot(
                jnp.concatenate([high, low], axis=0),
                right_of(b),
                preferred_element_type=jnp.float32,
            )
        sums = sums[: 2 * quarter] + sums[2 * quarter :]
    else:
        sums = jnp.zeros((2 * quarter, 2 * width), jnp.float32)
        for g in range(slots):
            active = jnp.where(g < loads[0], 1.0, 0.0)
            left = (left_of(diagrams[0, 0, g]) * active).astype(jnp.bfloat16)
            sums = sums + jnp.dot(
                left, right_of(diagrams[0, 1, g]), preferred_element_type=jnp.float32
            )
    scale = (width * slots) ** (-0.5)
    out[0, 0, 0] = (sums[:quarter, :width] - sums[quarter:, width:]) * scale
    out[0, 0, 1] = (sums[:quarter, width:] + sums[quarter:, :width]) * scale


    for part in range(PARTS):
        all_blocks(part).wait_send()


def on_device(n_sec, n_tp, n_blk, perambulator, backward, elementals, diagrams, owner_loads):
    rows, order = perambulator.shape[2:]
    width = elementals.shape[4]
    half = width // PARTS
    quarter = width // n_blk
    hbm = pl.BlockSpec(memory_space=pltpu.HBM)
    smem = pl.BlockSpec(memory_space=pltpu.SMEM)
    dma = pltpu.SemaphoreType.DMA
    return pl.pallas_call(
        functools.partial(kernel, n_sec, n_tp, n_blk),
        out_shape=jax.ShapeDtypeStruct((1, 1, 2, quarter, width), jnp.float32),
        in_specs=[hbm, hbm, hbm, smem, smem],
        out_specs=pl.BlockSpec(memory_space=pltpu.VMEM),
        scratch_shapes=[
            pltpu.VMEM((2, rows, order), jnp.bfloat16),
            pltpu.VMEM((2, order, rows), jnp.bfloat16),
            pltpu.VMEM((2, rows, width), jnp.bfloat16),
            pltpu.VMEM((PARTS, order, 2 * half), jnp.bfloat16),
            pltpu.VMEM((PARTS, rows, 2 * half), jnp.float32),
            pltpu.VMEM((PARTS, 2 * half, rows), jnp.float32),
            pltpu.VMEM((PARTS, 2 * half, rows), jnp.bfloat16),
            pltpu.VMEM((PARTS, 2 * half, rows), jnp.bfloat16),
            pltpu.VMEM((rows, 2 * width), jnp.bfloat16),
            pltpu.VMEM((PARTS, 2, half, width), jnp.bfloat16),
            pltpu.VMEM((PARTS, n_blk - 1, 2, half // n_blk, width), jnp.bfloat16),
            pltpu.VMEM((PARTS, n_tp * n_blk, 2, half // n_blk, width), jnp.bfloat16),
            dma((2, n_blk)),
            dma,
            dma((2, n_blk, PARTS, PIECES)),
            dma((2, n_blk, PARTS, PIECES)),
            dma((PARTS,)),
            dma((PARTS,)),
            dma((PARTS,)),
            dma((PARTS,)),
            dma((PARTS,)),
            dma((PARTS,)),
        ],
        compiler_params=pltpu.CompilerParams(
            collective_id=0, has_side_effects=True, vmem_limit_bytes=60 * 1024 * 1024
        ),
    )(perambulator, backward, elementals, jnp.swapaxes(diagrams, 1, 2), owner_loads)


def solution(mesh):
    placed = (
        P("tp", None, "blk", None),
        P("tp", None, None, "blk"),
        P("sec", "tp", None, "blk", None),
        P("tp", None, None),
        P("tp"),
    )
    sizes = (mesh.shape["sec"], mesh.shape["tp"], mesh.shape["blk"])
    return jax.shard_map(
        functools.partial(on_device, *sizes),
        mesh=mesh,
        in_specs=placed,
        out_specs=P("sec", "tp", None, "blk", None),
        check_vma=False,
    )
```

```python
import functools

import jax
import jax.numpy as jnp
from jax import lax
from jax.experimental import pallas as pl
from jax.experimental.pallas import tpu as pltpu
from jax.sharding import PartitionSpec as P

PARTS = 2
PIECES = 2
MESH = pl.DeviceIdType.MESH


def kernel(
    n_sec, n_tp, n_blk,
    tau_hbm, beta_hbm, tile_hbm, diagrams, loads, out,
    tau, beta, tile, gathered, image, conj_w, w_send, w_recv, image_full,
    partial, shares, blocks,
    load_sem, tile_sem, send_sem, recv_sem, w_send_sem, w_recv_sem,
    share_send_sem, share_recv_sem, block_send_sem, block_recv_sem,
):
    sec, tp, me = lax.axis_index("sec"), lax.axis_index("tp"), lax.axis_index("blk")
    rows, order = tau_hbm.shape[2], tau_hbm.shape[3]
    width = tile_hbm.shape[4]
    half = width // PARTS
    piece = rows // PIECES
    quarter = width // n_blk
    slots = diagrams.shape[2]

    both = jnp.minimum(me, n_blk - 1 - me)
    longer_below = me > n_blk - 1 - me

    def at_step(t):
        in_both = t <= 2 * both
        distance = jnp.where(in_both, lax.div(t + 1, 2), t - both)
        below = jnp.where(in_both, lax.rem(t, 2), jnp.where(longer_below, 1, 0))
        chunk = jnp.where(below == 1, me - distance, me + distance)
        return distance, below, chunk

    def rows_of(chunk):
        return pl.ds(pl.multiple_of(chunk * rows, rows), rows)

    def load(t):
        where = rows_of(at_step(t)[2])
        return (
            pltpu.make_async_copy(
                tau_hbm.at[0, :, :, where], tau.at[:, :, where], load_sem.at[0, t]
            ),
            pltpu.make_async_copy(
                beta_hbm.at[0, :, where, :], beta.at[:, where, :], load_sem.at[1, t]
            ),
        )

    own_tile = pltpu.make_async_copy(tile_hbm.at[0, 0], tile, tile_sem)
    own_tile.start()

    barrier = pltpu.get_barrier_semaphore()
    peers = n_tp * n_blk

    def each_peer(visit):
        def at(k):
            other_tp = lax.rem(tp + lax.div(k, n_blk), n_tp)
            other_blk = lax.rem(me + lax.rem(k, n_blk), n_blk)
            visit(other_tp, other_blk)

        if peers <= 16:
            for k in range(peers - 1, 0, -1):
                at(jnp.int32(k))
        else:
            lax.fori_loop(1, peers, lambda k, _: (at(k), 0)[1], 0)

    def greet(other_tp, other_blk):
        pl.semaphore_signal(
            barrier, inc=1, device_id=(sec, other_tp, other_blk), device_id_type=MESH
        )

    each_peer(greet)
    sec_next = lax.rem(sec + 1, n_sec)
    sec_back = lax.rem(sec + n_sec - 1, n_sec)
    greeted = peers - 1
    if n_sec > 1:
        pl.semaphore_signal(barrier, inc=1, device_id=(sec_next, tp, me), device_id_type=MESH)
        greeted += 1
    if n_sec > 2:
        pl.semaphore_signal(barrier, inc=1, device_id=(sec_back, tp, me), device_id_type=MESH)
        greeted += 1

    for t in range(n_blk):
        for copy in load(t):
            copy.start()

    own_tile.wait()
    lane = lax.broadcasted_iota(jnp.int32, (rows, width), 1)
    real = tile[0].astype(jnp.float32)
    imag = tile[1].astype(jnp.float32)
    gathered[0, rows_of(me), :] = jnp.where(
        lane < half, real, pltpu.roll(imag, half, 1)
    ).astype(jnp.bfloat16)
    gathered[1, rows_of(me), :] = jnp.where(
        lane < half, pltpu.roll(real, half, 1), imag
    ).astype(jnp.bfloat16)
    image[...] = jnp.zeros_like(image)
    dense = n_tp * n_tp <= slots
    if dense:
        counts = [[jnp.float32(0)] * n_tp for _ in range(n_tp)]
        for g in range(slots):
            left, right = diagrams[0, 0, g], diagrams[0, 1, g]
            live = g < loads[0]
            for a in range(n_tp):
                in_a = jnp.where(jnp.logical_and(live, left == a), 1.0, 0.0)
                for b in range(n_tp):
                    counts[a][b] = counts[a][b] + jnp.where(right == b, in_a, 0.0)
    conj_w[...] = jnp.zeros_like(conj_w)
    pl.semaphore_wait(barrier, greeted)

    def pass_on(upward, distance, part, r):
        chunk = jnp.where(upward == 1, me - distance, me + distance)
        target = jnp.where(upward == 1, me + 1, me - 1)
        where = pl.ds(pl.multiple_of(chunk * rows + r * piece, piece), piece)
        block = gathered.at[part, where, :]
        return pltpu.make_async_remote_copy(
            src_ref=block,
            dst_ref=block,
            send_sem=send_sem.at[upward, distance, part, r],
            recv_sem=recv_sem.at[upward, distance, part, r],
            device_id=(sec, tp, target),
            device_id_type=MESH,
        )

    def arrival(below, distance, part, r):
        chunk = jnp.where(below == 1, me - distance, me + distance)
        where = pl.ds(pl.multiple_of(chunk * rows + r * piece, piece), piece)
        block = gathered.at[part, where, :]
        return pltpu.make_async_remote_copy(
            src_ref=block,
            dst_ref=block,
            send_sem=send_sem.at[below, distance, part, r],
            recv_sem=recv_sem.at[below, distance - 1, part, r],
            device_id=(sec, tp, me),
            device_id_type=MESH,
        )

    def send_own(upward, part):
        for r in range(PIECES):
            pass_on(upward, 0, part, r).start()

    for part in range(PARTS):
        @pl.when(me < n_blk - 1)
        def _():
            send_own(1, part)

        @pl.when(me > 0)
        def _():
            send_own(0, part)

    def w_copy(part):
        return pltpu.make_async_remote_copy(
            src_ref=w_send.at[part],
            dst_ref=w_recv.at[part],
            send_sem=w_send_sem.at[part],
            recv_sem=w_recv_sem.at[part],
            device_id=(sec_next, tp, me),
            device_id_type=MESH,
        )

    piece_lane = lax.broadcasted_iota(jnp.int32, (piece, width), 1)
    for part in range(PARTS):
        def receive(u):
            t, r = lax.div(u, PIECES), lax.rem(u, PIECES)
            distance, below, chunk = at_step(t)

            @pl.when(jnp.logical_and(t > 0, u < n_blk * PIECES))
            def _():
                arrival(below, distance, part, r).wait_recv()
                more = jnp.where(below == 1, me < n_blk - 1, me > 0)

                @pl.when(more)
                def _():
                    pass_on(below, distance, part, r).start()

        def step(u, _):
            t, r = lax.div(u, PIECES), lax.rem(u, PIECES)
            chunk = at_step(t)[2]

            @pl.when(both > 0)
            def _():
                receive(u + 1)

            if part == 0:
                @pl.when(r == 0)
                def _():
                    for copy in load(t):
                        copy.wait()

            where = pl.ds(pl.multiple_of(chunk * rows + r * piece, piece), piece)
            straight = gathered[part, where, :]
            upright = straight.T
            upright = jnp.concatenate(
                [upright, jnp.concatenate([upright[half:], -upright[:half]], axis=0)], axis=1
            )
            conj_w[part] += jnp.dot(
                upright,
                jnp.concatenate([beta[0, where, :], beta[1, where, :]], axis=0),
                preferred_element_type=jnp.float32,
            )

            @pl.when(u == n_blk * PIECES - 1)
            def _():
                if n_sec > 1:
                    w_send[part] = conj_w[part].astype(jnp.bfloat16)
                    w_copy(part).start()
                else:
                    w_recv[part] = conj_w[part].astype(jnp.bfloat16)

            turned = pltpu.roll(straight.astype(jnp.float32), half, 1)
            crossed = jnp.where(piece_lane < half, -turned, turned).astype(jnp.bfloat16)
            image[part] += jnp.dot(
                jnp.concatenate([tau[0, :, where], tau[1, :, where]], axis=1),
                jnp.concatenate([straight, crossed], axis=0),
                preferred_element_type=jnp.float32,
            )

            @pl.when(both == 0)
            def _():
                receive(u + 1)

            return 0

        lax.fori_loop(0, n_blk * PIECES, step, 0)

    first, second = image[0], image[1]
    image_full[:, :width] = jnp.where(
        lane < half, first, pltpu.roll(second, half, 1)
    ).astype(jnp.bfloat16)
    image_full[:, width:] = jnp.where(
        lane < half, pltpu.roll(first, half, 1), second
    ).astype(jnp.bfloat16)

    share = half // n_blk

    def share_copy(part, distance):
        target = lax.rem(me + distance, n_blk)
        where = pl.ds(pl.multiple_of(target * share, share), share)
        return pltpu.make_async_remote_copy(
            src_ref=partial.at[part, :, where, :],
            dst_ref=shares.at[part, distance - 1],
            send_sem=share_send_sem.at[part],
            recv_sem=share_recv_sem.at[part],
            device_id=(sec, tp, target),
            device_id_type=MESH,
        )

    def all_shares(part):
        every = shares.at[part]
        return pltpu.make_async_remote_copy(
            src_ref=every,
            dst_ref=every,
            send_sem=share_send_sem.at[part],
            recv_sem=share_recv_sem.at[part],
            device_id=(sec, tp, me),
            device_id_type=MESH,
        )

    def block_copy(part, slot, other_tp, other_blk):
        return pltpu.make_async_remote_copy(
            src_ref=slot,
            dst_ref=slot,
            send_sem=block_send_sem.at[part],
            recv_sem=block_recv_sem.at[part],
            device_id=(sec, other_tp, other_blk),
            device_id_type=MESH,
        )

    def all_blocks(part):
        return block_copy(part, blocks.at[part, pl.ds(0, peers - 1)], tp, me)

    def start_sum(part):
        if n_sec > 1:
            w_copy(part).wait_recv()
        product = jnp.dot(w_recv[part], image_full[...], preferred_element_type=jnp.float32)
        partial[part, 0] = (product[:half, :width] + product[half:, width:]).astype(jnp.bfloat16)
        partial[part, 1] = (product[:half, width:] - product[half:, :width]).astype(jnp.bfloat16)
        for distance in range(1, n_blk):
            share_copy(part, distance).start()

    def end_sum(part):
        where = pl.ds(pl.multiple_of(me * share, share), share)
        total = partial[part, :, where, :].astype(jnp.float32)
        all_shares(part).wait_recv()
        for distance in range(1, n_blk):
            total = total + shares[part, distance - 1].astype(jnp.float32)
        own = tp * n_blk + me
        blocks[part, own] = (total * order ** (-0.5)).astype(jnp.bfloat16)
        each_peer(lambda *other: block_copy(part, blocks.at[part, own], *other).start())

    start_sum(0)
    for part in range(PARTS):
        end_sum(part)
        if part + 1 < PARTS:
            start_sum(part + 1)

    def drain(u, _):
        distance = lax.div(u, PIECES)
        r = lax.rem(u, PIECES)
        for part in range(PARTS):
            @pl.when(jnp.logical_and(distance <= me, me < n_blk - 1))
            def _():
                pass_on(1, distance, part, r).wait_send()

            @pl.when(jnp.logical_and(me + distance < n_blk, me > 0))
            def _():
                pass_on(0, distance, part, r).wait_send()

        return 0

    lax.fori_loop(0, n_blk * PIECES, drain, 0)
    if n_sec > 1:
        for part in range(PARTS):
            w_copy(part).wait_send()
    for part in range(PARTS):
        all_shares(part).wait_send()
    for part in range(PARTS):
        all_blocks(part).wait_recv()

    def right_of(index):
        first = index * n_blk
        right = blocks[:, pl.ds(first, n_blk)].reshape(PARTS * n_blk, 2, share, width)
        return jnp.concatenate(
            [right[:, 0].reshape(width, width), right[:, 1].reshape(width, width)], axis=1
        )

    def left_of(index):
        first = me * PARTS
        at = index * n_blk + lax.rem(first, n_blk)
        left = blocks[lax.div(first, n_blk), pl.ds(at, PARTS)].astype(jnp.float32)
        return jnp.concatenate(
            [left[:, 0].reshape(quarter, width), left[:, 1].reshape(quarter, width)], axis=0
        )

    if dense:
        lefts = [left_of(a) for a in range(n_tp)]
        sums = jnp.zeros((4 * quarter, 2 * width), jnp.float32)
        for b in range(n_tp):
            left = lefts[0] * counts[0][b]
            for a in range(1, n_tp):
                left = left + lefts[a] * counts[a][b]
            high = left.astype(jnp.bfloat16)
            low = (left - high.astype(jnp.float32)).astype(jnp.bfloat16)
            sums = sums + jnp.dot(
                jnp.concatenate([high, low], axis=0),
                right_of(b),
                preferred_element_type=jnp.float32,
            )
        sums = sums[: 2 * quarter] + sums[2 * quarter :]
    else:
        sums = jnp.zeros((2 * quarter, 2 * width), jnp.float32)
        for g in range(slots):
            active = jnp.where(g < loads[0], 1.0, 0.0)
            left = (left_of(diagrams[0, 0, g]) * active).astype(jnp.bfloat16)
            sums = sums + jnp.dot(
                left, right_of(diagrams[0, 1, g]), preferred_element_type=jnp.float32
            )
    scale = (width * slots) ** (-0.5)
    out[0, 0, 0] = (sums[:quarter, :width] - sums[quarter:, width:]) * scale
    out[0, 0, 1] = (sums[:quarter, width:] + sums[quarter:, :width]) * scale


    for part in range(PARTS):
        all_blocks(part).wait_send()


def on_device(n_sec, n_tp, n_blk, perambulator, backward, elementals, diagrams, owner_loads):
    rows, order = perambulator.shape[2:]
    width = elementals.shape[4]
    half = width // PARTS
    quarter = width // n_blk
    hbm = pl.BlockSpec(memory_space=pltpu.HBM)
    smem = pl.BlockSpec(memory_space=pltpu.SMEM)
    dma = pltpu.SemaphoreType.DMA
    return pl.pallas_call(
        functools.partial(kernel, n_sec, n_tp, n_blk),
        out_shape=jax.ShapeDtypeStruct((1, 1, 2, quarter, width), jnp.float32),
        in_specs=[hbm, hbm, hbm, smem, smem],
        out_specs=pl.BlockSpec(memory_space=pltpu.VMEM),
        scratch_shapes=[
            pltpu.VMEM((2, rows, order), jnp.bfloat16),
            pltpu.VMEM((2, order, rows), jnp.bfloat16),
            pltpu.VMEM((2, rows, width), jnp.bfloat16),
            pltpu.VMEM((PARTS, order, 2 * half), jnp.bfloat16),
            pltpu.VMEM((PARTS, rows, 2 * half), jnp.float32),
            pltpu.VMEM((PARTS, 2 * half, rows), jnp.float32),
            pltpu.VMEM((PARTS, 2 * half, rows), jnp.bfloat16),
            pltpu.VMEM((PARTS, 2 * half, rows), jnp.bfloat16),
            pltpu.VMEM((rows, 2 * width), jnp.bfloat16),
            pltpu.VMEM((PARTS, 2, half, width), jnp.bfloat16),
            pltpu.VMEM((PARTS, n_blk - 1, 2, half // n_blk, width), jnp.bfloat16),
            pltpu.VMEM((PARTS, n_tp * n_blk, 2, half // n_blk, width), jnp.bfloat16),
            dma((2, n_blk)),
            dma,
            dma((2, n_blk, PARTS, PIECES)),
            dma((2, n_blk, PARTS, PIECES)),
            dma((PARTS,)),
            dma((PARTS,)),
            dma((PARTS,)),
            dma((PARTS,)),
            dma((PARTS,)),
            dma((PARTS,)),
        ],
        compiler_params=pltpu.CompilerParams(
            collective_id=0, has_side_effects=True, vmem_limit_bytes=60 * 1024 * 1024
        ),
    )(perambulator, backward, elementals, jnp.swapaxes(diagrams, 1, 2), owner_loads)


def solution(mesh):
    placed = (
        P("tp", None, "blk", None),
        P("tp", None, None, "blk"),
        P("sec", "tp", None, "blk", None),
        P("tp", None, None),
        P("tp"),
    )
    sizes = (mesh.shape["sec"], mesh.shape["tp"], mesh.shape["blk"])
    return jax.shard_map(
        functools.partial(on_device, *sizes),
        mesh=mesh,
        in_specs=placed,
        out_specs=P("sec", "tp", None, "blk", None),
        check_vma=False,
    )
```

```python
import functools

import jax
import jax.numpy as jnp
from jax import lax
from jax.experimental import pallas as pl
from jax.experimental.pallas import tpu as pltpu
from jax.sharding import PartitionSpec as P

PARTS = 2
PIECES = 2
MESH = pl.DeviceIdType.MESH


def kernel(
    n_sec, n_tp, n_blk,
    tau_hbm, beta_hbm, tile_hbm, diagrams, loads, out,
    tau, beta, tile, gathered, image, conj_w, w_send, w_recv, image_full,
    partial, shares, blocks,
    load_sem, tile_sem, send_sem, recv_sem, w_send_sem, w_recv_sem,
    share_send_sem, share_recv_sem, block_send_sem, block_recv_sem,
):
    sec, tp, me = lax.axis_index("sec"), lax.axis_index("tp"), lax.axis_index("blk")
    rows, order = tau_hbm.shape[2], tau_hbm.shape[3]
    width = tile_hbm.shape[4]
    half = width // PARTS
    piece = rows // PIECES
    quarter = width // n_blk
    slots = diagrams.shape[2]

    both = jnp.minimum(me, n_blk - 1 - me)
    longer_below = me > n_blk - 1 - me

    def at_step(t):
        in_both = t <= 2 * both
        distance = jnp.where(in_both, lax.div(t + 1, 2), t - both)
        below = jnp.where(in_both, lax.rem(t, 2), jnp.where(longer_below, 1, 0))
        chunk = jnp.where(below == 1, me - distance, me + distance)
        return distance, below, chunk

    def rows_of(chunk):
        return pl.ds(pl.multiple_of(chunk * rows, rows), rows)

    def load(t):
        where = rows_of(at_step(t)[2])
        return (
            pltpu.make_async_copy(
                tau_hbm.at[0, :, :, where], tau.at[:, :, where], load_sem.at[0, t]
            ),
            pltpu.make_async_copy(
                beta_hbm.at[0, :, where, :], beta.at[:, where, :], load_sem.at[1, t]
            ),
        )

    own_tile = pltpu.make_async_copy(tile_hbm.at[0, 0], tile, tile_sem)
    own_tile.start()

    barrier = pltpu.get_barrier_semaphore()
    peers = n_tp * n_blk

    def each_peer(visit):
        def at(k):
            other_tp = lax.rem(tp + lax.div(k, n_blk), n_tp)
            other_blk = lax.rem(me + lax.rem(k, n_blk), n_blk)
            visit(other_tp, other_blk)

        if peers <= 16:
            for k in range(peers - 1, 0, -1):
                at(jnp.int32(k))
        else:
            lax.fori_loop(1, peers, lambda k, _: (at(k), 0)[1], 0)

    def greet(other_tp, other_blk):
        pl.semaphore_signal(
            barrier, inc=1, device_id=(sec, other_tp, other_blk), device_id_type=MESH
        )

    each_peer(greet)
    sec_next = lax.rem(sec + 1, n_sec)
    sec_back = lax.rem(sec + n_sec - 1, n_sec)
    greeted = peers - 1
    if n_sec > 1:
        pl.semaphore_signal(barrier, inc=1, device_id=(sec_next, tp, me), device_id_type=MESH)
        greeted += 1
    if n_sec > 2:
        pl.semaphore_signal(barrier, inc=1, device_id=(sec_back, tp, me), device_id_type=MESH)
        greeted += 1

    for t in range(n_blk):
        for copy in load(t):
            copy.start()

    own_tile.wait()
    lane = lax.broadcasted_iota(jnp.int32, (rows, width), 1)
    real = tile[0].astype(jnp.float32)
    imag = tile[1].astype(jnp.float32)
    gathered[0, rows_of(me), :] = jnp.where(
        lane < half, real, pltpu.roll(imag, half, 1)
    ).astype(jnp.bfloat16)
    gathered[1, rows_of(me), :] = jnp.where(
        lane < half, pltpu.roll(real, half, 1), imag
    ).astype(jnp.bfloat16)
    image[...] = jnp.zeros_like(image)
    dense = n_tp * n_tp <= slots
    if dense:
        counts = [[jnp.float32(0)] * n_tp for _ in range(n_tp)]
        for g in range(slots):
            left, right = diagrams[0, 0, g], diagrams[0, 1, g]
            live = g < loads[0]
            for a in range(n_tp):
                in_a = jnp.where(jnp.logical_and(live, left == a), 1.0, 0.0)
                for b in range(n_tp):
                    counts[a][b] = counts[a][b] + jnp.where(right == b, in_a, 0.0)
    conj_w[...] = jnp.zeros_like(conj_w)
    pl.semaphore_wait(barrier, greeted)

    def pass_on(upward, distance, part, r):
        chunk = jnp.where(upward == 1, me - distance, me + distance)
        target = jnp.where(upward == 1, me + 1, me - 1)
        where = pl.ds(pl.multiple_of(chunk * rows + r * piece, piece), piece)
        block = gathered.at[part, where, :]
        return pltpu.make_async_remote_copy(
            src_ref=block,
            dst_ref=block,
            send_sem=send_sem.at[upward, distance, part, r],
            recv_sem=recv_sem.at[upward, distance, part, r],
            device_id=(sec, tp, target),
            device_id_type=MESH,
        )

    def arrival(below, distance, part, r):
        chunk = jnp.where(below == 1, me - distance, me + distance)
        where = pl.ds(pl.multiple_of(chunk * rows + r * piece, piece), piece)
        block = gathered.at[part, where, :]
        return pltpu.make_async_remote_copy(
            src_ref=block,
            dst_ref=block,
            send_sem=send_sem.at[below, distance, part, r],
            recv_sem=recv_sem.at[below, distance - 1, part, r],
            device_id=(sec, tp, me),
            device_id_type=MESH,
        )

    def send_own(upward, part):
        for r in range(PIECES):
            pass_on(upward, 0, part, r).start()

    for part in range(PARTS):
        @pl.when(me < n_blk - 1)
        def _():
            send_own(1, part)

        @pl.when(me > 0)
        def _():
            send_own(0, part)

    def w_copy(part):
        return pltpu.make_async_remote_copy(
            src_ref=w_send.at[part],
            dst_ref=w_recv.at[part],
            send_sem=w_send_sem.at[part],
            recv_sem=w_recv_sem.at[part],
            device_id=(sec_next, tp, me),
            device_id_type=MESH,
        )

    piece_lane = lax.broadcasted_iota(jnp.int32, (piece, width), 1)
    for part in range(PARTS):
        def receive(u):
            t, r = lax.div(u, PIECES), lax.rem(u, PIECES)
            distance, below, chunk = at_step(t)

            @pl.when(jnp.logical_and(t > 0, u < n_blk * PIECES))
            def _():
                arrival(below, distance, part, r).wait_recv()
                more = jnp.where(below == 1, me < n_blk - 1, me > 0)

                @pl.when(more)
                def _():
                    pass_on(below, distance, part, r).start()

        def step(u, _):
            t, r = lax.div(u, PIECES), lax.rem(u, PIECES)
            chunk = at_step(t)[2]

            @pl.when(both > 0)
            def _():
                receive(u + 1)

            if part == 0:
                @pl.when(r == 0)
                def _():
                    for copy in load(t):
                        copy.wait()

            where = pl.ds(pl.multiple_of(chunk * rows + r * piece, piece), piece)
            straight = gathered[part, where, :]
            wide = straight.astype(jnp.float32)
            turned = pltpu.roll(wide, half, 1)
            turned = jnp.where(piece_lane < half, -turned, turned)
            crossed = turned.astype(jnp.bfloat16)
            conj_w[part] += jnp.dot(
                wide.T.astype(jnp.bfloat16),
                beta[0, where, :],
                preferred_element_type=jnp.float32,
            ) + jnp.dot(
                (-turned).T.astype(jnp.bfloat16),
                beta[1, where, :],
                preferred_element_type=jnp.float32,
            )

            @pl.when(u == n_blk * PIECES - 1)
            def _():
                if n_sec > 1:
                    w_send[part] = conj_w[part].astype(jnp.bfloat16)
                    w_copy(part).start()
                else:
                    w_recv[part] = conj_w[part].astype(jnp.bfloat16)

            image[part] += jnp.dot(
                tau[0, :, where], straight, preferred_element_type=jnp.float32
            ) + jnp.dot(tau[1, :, where], crossed, preferred_element_type=jnp.float32)

            @pl.when(both == 0)
            def _():
                receive(u + 1)

            return 0

        lax.fori_loop(0, n_blk * PIECES, step, 0)

    first, second = image[0], image[1]
    image_full[:, :width] = jnp.where(
        lane < half, first, pltpu.roll(second, half, 1)
    ).astype(jnp.bfloat16)
    image_full[:, width:] = jnp.where(
        lane < half, pltpu.roll(first, half, 1), second
    ).astype(jnp.bfloat16)

    share = half // n_blk

    def share_copy(part, distance):
        target = lax.rem(me + distance, n_blk)
        where = pl.ds(pl.multiple_of(target * share, share), share)
        return pltpu.make_async_remote_copy(
            src_ref=partial.at[part, :, where, :],
            dst_ref=shares.at[part, distance - 1],
            send_sem=share_send_sem.at[part],
            recv_sem=share_recv_sem.at[part],
            device_id=(sec, tp, target),
            device_id_type=MESH,
        )

    def all_shares(part):
        every = shares.at[part]
        return pltpu.make_async_remote_copy(
            src_ref=every,
            dst_ref=every,
            send_sem=share_send_sem.at[part],
            recv_sem=share_recv_sem.at[part],
            device_id=(sec, tp, me),
            device_id_type=MESH,
        )

    def block_copy(part, slot, other_tp, other_blk):
        return pltpu.make_async_remote_copy(
            src_ref=slot,
            dst_ref=slot,
            send_sem=block_send_sem.at[part],
            recv_sem=block_recv_sem.at[part],
            device_id=(sec, other_tp, other_blk),
            device_id_type=MESH,
        )

    def all_blocks(part):
        return block_copy(part, blocks.at[part, pl.ds(0, peers - 1)], tp, me)

    def start_sum(part):
        if n_sec > 1:
            w_copy(part).wait_recv()
        product = jnp.dot(w_recv[part], image_full[...], preferred_element_type=jnp.float32)
        partial[part, 0] = (product[:half, :width] + product[half:, width:]).astype(jnp.bfloat16)
        partial[part, 1] = (product[:half, width:] - product[half:, :width]).astype(jnp.bfloat16)
        for distance in range(1, n_blk):
            share_copy(part, distance).start()

    def end_sum(part):
        where = pl.ds(pl.multiple_of(me * share, share), share)
        total = partial[part, :, where, :].astype(jnp.float32)
        all_shares(part).wait_recv()
        for distance in range(1, n_blk):
            total = total + shares[part, distance - 1].astype(jnp.float32)
        own = tp * n_blk + me
        blocks[part, own] = (total * order ** (-0.5)).astype(jnp.bfloat16)
        each_peer(lambda *other: block_copy(part, blocks.at[part, own], *other).start())

    start_sum(0)
    for part in range(PARTS):
        end_sum(part)
        if part + 1 < PARTS:
            start_sum(part + 1)

    def drain(u, _):
        distance = lax.div(u, PIECES)
        r = lax.rem(u, PIECES)
        for part in range(PARTS):
            @pl.when(jnp.logical_and(distance <= me, me < n_blk - 1))
            def _():
                pass_on(1, distance, part, r).wait_send()

            @pl.when(jnp.logical_and(me + distance < n_blk, me > 0))
            def _():
                pass_on(0, distance, part, r).wait_send()

        return 0

    lax.fori_loop(0, n_blk * PIECES, drain, 0)
    if n_sec > 1:
        for part in range(PARTS):
            w_copy(part).wait_send()
    for part in range(PARTS):
        all_shares(part).wait_send()
    for part in range(PARTS):
        all_blocks(part).wait_recv()

    def right_of(index):
        first = index * n_blk
        right = blocks[:, pl.ds(first, n_blk)].reshape(PARTS * n_blk, 2, share, width)
        return jnp.concatenate(
            [right[:, 0].reshape(width, width), right[:, 1].reshape(width, width)], axis=1
        )

    def left_of(index):
        first = me * PARTS
        at = index * n_blk + lax.rem(first, n_blk)
        left = blocks[lax.div(first, n_blk), pl.ds(at, PARTS)].astype(jnp.float32)
        return jnp.concatenate(
            [left[:, 0].reshape(quarter, width), left[:, 1].reshape(quarter, width)], axis=0
        )

    if dense:
        lefts = [left_of(a) for a in range(n_tp)]
        sums = jnp.zeros((4 * quarter, 2 * width), jnp.float32)
        for b in range(n_tp):
            left = lefts[0] * counts[0][b]
            for a in range(1, n_tp):
                left = left + lefts[a] * counts[a][b]
            high = left.astype(jnp.bfloat16)
            low = (left - high.astype(jnp.float32)).astype(jnp.bfloat16)
            sums = sums + jnp.dot(
                jnp.concatenate([high, low], axis=0),
                right_of(b),
                preferred_element_type=jnp.float32,
            )
        sums = sums[: 2 * quarter] + sums[2 * quarter :]
    else:
        sums = jnp.zeros((2 * quarter, 2 * width), jnp.float32)
        for g in range(slots):
            active = jnp.where(g < loads[0], 1.0, 0.0)
            left = (left_of(diagrams[0, 0, g]) * active).astype(jnp.bfloat16)
            sums = sums + jnp.dot(
                left, right_of(diagrams[0, 1, g]), preferred_element_type=jnp.float32
            )
    scale = (width * slots) ** (-0.5)
    out[0, 0, 0] = (sums[:quarter, :width] - sums[quarter:, width:]) * scale
    out[0, 0, 1] = (sums[:quarter, width:] + sums[quarter:, :width]) * scale


    for part in range(PARTS):
        all_blocks(part).wait_send()


def on_device(n_sec, n_tp, n_blk, perambulator, backward, elementals, diagrams, owner_loads):
    rows, order = perambulator.shape[2:]
    width = elementals.shape[4]
    half = width // PARTS
    quarter = width // n_blk
    hbm = pl.BlockSpec(memory_space=pltpu.HBM)
    smem = pl.BlockSpec(memory_space=pltpu.SMEM)
    dma = pltpu.SemaphoreType.DMA
    return pl.pallas_call(
        functools.partial(kernel, n_sec, n_tp, n_blk),
        out_shape=jax.ShapeDtypeStruct((1, 1, 2, quarter, width), jnp.float32),
        in_specs=[hbm, hbm, hbm, smem, smem],
        out_specs=pl.BlockSpec(memory_space=pltpu.VMEM),
        scratch_shapes=[
            pltpu.VMEM((2, rows, order), jnp.bfloat16),
            pltpu.VMEM((2, order, rows), jnp.bfloat16),
            pltpu.VMEM((2, rows, width), jnp.bfloat16),
            pltpu.VMEM((PARTS, order, 2 * half), jnp.bfloat16),
            pltpu.VMEM((PARTS, rows, 2 * half), jnp.float32),
            pltpu.VMEM((PARTS, 2 * half, rows), jnp.float32),
            pltpu.VMEM((PARTS, 2 * half, rows), jnp.bfloat16),
            pltpu.VMEM((PARTS, 2 * half, rows), jnp.bfloat16),
            pltpu.VMEM((rows, 2 * width), jnp.bfloat16),
            pltpu.VMEM((PARTS, 2, half, width), jnp.bfloat16),
            pltpu.VMEM((PARTS, n_blk - 1, 2, half // n_blk, width), jnp.bfloat16),
            pltpu.VMEM((PARTS, n_tp * n_blk, 2, half // n_blk, width), jnp.bfloat16),
            dma((2, n_blk)),
            dma,
            dma((2, n_blk, PARTS, PIECES)),
            dma((2, n_blk, PARTS, PIECES)),
            dma((PARTS,)),
            dma((PARTS,)),
            dma((PARTS,)),
            dma((PARTS,)),
            dma((PARTS,)),
            dma((PARTS,)),
        ],
        compiler_params=pltpu.CompilerParams(
            collective_id=0, has_side_effects=True, vmem_limit_bytes=60 * 1024 * 1024
        ),
    )(perambulator, backward, elementals, jnp.swapaxes(diagrams, 1, 2), owner_loads)


def solution(mesh):
    placed = (
        P("tp", None, "blk", None),
        P("tp", None, None, "blk"),
        P("sec", "tp", None, "blk", None),
        P("tp", None, None),
        P("tp"),
    )
    sizes = (mesh.shape["sec"], mesh.shape["tp"], mesh.shape["blk"])
    return jax.shard_map(
        functools.partial(on_device, *sizes),
        mesh=mesh,
        in_specs=placed,
        out_specs=P("sec", "tp", None, "blk", None),
        check_vma=False,
    )
```
